1024 devices in a mesh: dp: 64 (over z, core), dap: 16 (over y, x).
Axes of the slice: x: 4, y: 4, z: 32, core: 2. Of those that a mesh axis runs over, the one named last changes fastest.
Arguments:
- pair_rep: bfloat16 [8192, 128, 128], P(('dp', 'dap')), parts along dimension 0, may hold values from -6 to 6
- proj_weight: bfloat16 [2, 128, 512], replicated, may hold values from -0.5 to 0.5
- gate_weight: bfloat16 [2, 128, 128], replicated, may hold values from -0.5 to 0.5
- out_weight: bfloat16 [2, 128, 128], replicated, may hold values from -0.5 to 0.5
- norm_gain: float32 [2, 128], replicated, may hold values from 0.25 to 1.75
- mid_gain: float32 [2, 128], replicated, may hold values from 0.25 to 1.75
Outputs:
- pair_out: bfloat16 [8192, 128, 128], P(('dp', 'dap')), parts along dimension 0
The draws below stay inside these ranges and needn't reach their ends.
There are 64 independent parts, one for each index of `dp`. The reference program is written for one: setup_inputs(seed, part) draws one part's arguments, and reference() takes and returns one part's arrays. A program takes and returns all parts, laid end to end along the dimension named above; an argument that names none is the same for every part. Nothing has to cross between parts.
All inputs are finite; a program needn't handle non-finite values.
Results may differ from the reference program's by a relative error of at most 0.017.
Values may be sent and summed in bfloat16 or wider, within the bound.
A program may use at most 32 MiB of HBM per device.

```python
import jax
import jax.numpy as jnp
from jax import lax

C = 128
H = 128
RES = 128


def levels(own_key, extent, cuts, low, top_value):
    factor_of = 1.0
    for dim, parts in cuts:
        draws = jax.random.uniform(jax.random.fold_in(jax.random.fold_in(own_key, 6), dim), (parts,), jnp.float32, low / len(cuts), top_value / len(cuts))
        factor_of = factor_of * jnp.repeat(jnp.exp(draws), extent[dim] // parts).reshape((-1,) + (1,) * (len(extent) - 1 - dim))
    return factor_of


def noise(stream_key, extent, deviation, reach, pieces=(), kind=jnp.bfloat16):
    level = levels(stream_key, extent, pieces, -0.22, 0.18) if pieces else 1.0
    values = jax.random.normal(stream_key, extent, jnp.float32) * deviation * level
    return jnp.minimum(jnp.maximum(values, -reach), reach).astype(kind)


def setup_inputs(seed: int = 0, part: int = 0) -> dict:
    seeds = jax.random.split(jax.random.key(seed), 7)
    part_splits = jax.random.split(jax.random.fold_in(seeds[6], part), 7)
    return {
        "pair_rep": noise(part_splits[0], (RES, RES, C), 1.0, 6.0, ((0, 16),)),
        "proj_weight": noise(seeds[1], (2, C, 4 * H), C ** -0.5, 0.5),
        "gate_weight": noise(seeds[2], (2, C, C), C ** -0.5, 0.5),
        "out_weight": noise(seeds[3], (2, H, C), H ** -0.5, 0.5),
        "norm_gain": jnp.clip(1.0 + 0.15 * jax.random.normal(seeds[4], (2, C), jnp.float32), 0.25, 1.75),
        "mid_gain": jnp.clip(1.0 + 0.15 * jax.random.normal(seeds[5], (2, H), jnp.float32), 0.25, 1.75),
    }


def normalize(values, gain):
    mean = lax.optimization_barrier(jnp.mean(values, axis=-1, keepdims=True))
    centered = values - mean
    var = lax.optimization_barrier(jnp.mean(centered * centered, axis=-1, keepdims=True))
    return centered * jax.lax.rsqrt(var + 1e-05) * gain

def triangle(pair_in, proj_w, gate_w, out_w, gain_in, gain_mid, incoming):
    size = pair_in.shape[0]
    chans = pair_in.shape[2]
    hidden = out_w.shape[0]
    normed = normalize(pair_in.astype(jnp.float32), gain_in).astype(jnp.bfloat16)
    flat = normed.reshape(-1, chans)
    proj = jnp.dot(flat, proj_w, preferred_element_type=jnp.float32).reshape(size, size, 4 * hidden)
    left_proj = (jax.nn.sigmoid(proj[..., hidden:2 * hidden]) * proj[..., :hidden]).astype(jnp.bfloat16)
    right_proj = (jax.nn.sigmoid(proj[..., 3 * hidden:]) * proj[..., 2 * hidden:3 * hidden]).astype(jnp.bfloat16)
    if incoming:
        mixed = jnp.einsum('kic,kjc->ijc', left_proj.astype(jnp.float32), right_proj.astype(jnp.float32))
    else:
        mixed = jnp.einsum('ikc,jkc->ijc', left_proj.astype(jnp.float32), right_proj.astype(jnp.float32))
    mid = normalize(mixed, gain_mid).astype(jnp.bfloat16)
    gate = jax.nn.sigmoid(jnp.dot(flat, gate_w, preferred_element_type=jnp.float32))
    update = gate * jnp.dot(mid.reshape(-1, hidden), out_w, preferred_element_type=jnp.float32)
    return (pair_in.astype(jnp.float32) + update.reshape(size, size, chans)).astype(jnp.bfloat16)

def reference(pair_rep, proj_weight, gate_weight, out_weight, norm_gain, mid_gain):
    after_out = triangle(pair_rep, proj_weight[0], gate_weight[0], out_weight[0], norm_gain[0], mid_gain[0], False)
    return triangle(after_out, proj_weight[1], gate_weight[1], out_weight[1], norm_gain[1], mid_gain[1], True)
```

```python
import jax
import jax.numpy as jnp
from jax import lax
from jax.experimental import pallas as pl
from jax.experimental.pallas import tpu as pltpu
from jax.sharding import PartitionSpec as P

MESH = pl.DeviceIdType.MESH
BF16 = jnp.bfloat16
F32 = jnp.float32
SIDE = 4
GROUP = SIDE * SIDE
RES = 128
CHANS = 128
ROWS = RES // GROUP
OWN = CHANS // GROUP


def far_first(offset):
    return -sum(min(step, SIDE - step) for step in offset)


OFFSETS = sorted(
    [(dy, dx) for dy in range(SIDE) for dx in range(SIDE) if (dy, dx) != (0, 0)], key=far_first
)


def contract(lhs, rhs, lhs_dim, rhs_dim):
    return lax.dot_general(
        lhs, rhs, (((lhs_dim,), (rhs_dim,)), ((), ())), preferred_element_type=F32
    )


def kernel(
    pair, proj_w, gate_w, out_w, norm_gain, mid_gain, result,
    proj_t, gate_t, out_t, gains, chan_pair, chan_normed, chan_gate, row_gate, row_pair,
    send_proj, recv_proj, send_mix, recv_mix, wide_proj, wide_mix, stats, send_sem, recv_sem,
):
    crop = lax.axis_index("dp")
    me = lax.axis_index("dap")
    y, x = me // SIDE, lax.rem(me, SIDE)

    def towards(offset):
        return lax.rem(y + offset[0], SIDE) * SIDE + lax.rem(x + offset[1], SIDE)

    def back(offset):
        return towards((SIDE - offset[0], SIDE - offset[1]))

    barrier = pltpu.get_barrier_semaphore()
    for offset in OFFSETS:
        pl.semaphore_signal(
            barrier, inc=1, device_id=(crop, towards(offset)), device_id_type=MESH
        )

    def exchange(phase, source, target):
        copies = []
        for n, offset in enumerate(OFFSETS):
            there = towards(offset)
            copy = pltpu.make_async_remote_copy(
                src_ref=source.at[there],
                dst_ref=target.at[me],
                send_sem=send_sem.at[phase, n],
                recv_sem=recv_sem.at[phase, n],
                device_id=(crop, there),
                device_id_type=MESH,
            )
            copy.start()
            copies.append(copy)
        return copies

    def column(row):
        return jnp.broadcast_to(row, (CHANS, CHANS)).T

    def turn_projection(block):
        for part in range(4):
            piece = proj_w[block, :, part * CHANS : (part + 1) * CHANS].astype(F32)
            proj_t[block, part] = (piece.T * 0.5).astype(BF16)

    def project(block, step, values):
        mean = jnp.mean(values, axis=0, keepdims=True)
        centered = values - mean
        var = jnp.mean(centered * centered, axis=0, keepdims=True)
        gain = gains[block]
        normed = centered * lax.rsqrt(var + 1e-05) * jnp.concatenate([gain, gain], axis=1)
        normed = normed.astype(BF16)
        chan_normed[:, step * 256 : (step + 1) * 256] = normed
        sides = []
        for side in range(2):
            half_value = contract(proj_t[block, 2 * side], normed, 1, 0)
            half_gate = contract(proj_t[block, 2 * side + 1], normed, 1, 0)
            sides.append(half_value * jnp.tanh(half_gate) + half_value)
        for h in range(2):
            parts = [s[:, h * RES : (h + 1) * RES].reshape(GROUP, OWN, RES) for s in sides]
            send_proj[block, :, 2 * step + h] = jnp.concatenate(parts, axis=1).astype(BF16)

    def widen(block, source, origin):
        wide_proj[pl.ds(pl.multiple_of(origin * RES, RES), RES), :] = (
            source[...].astype(F32).reshape(RES, RES)
        )

    def mix(block, copies):
        widen(block, send_proj.at[block, me], me)
        for n, offset in enumerate(OFFSETS):
            copies[n].wait_recv()
            origin = back(offset)
            widen(block, recv_proj.at[block, origin], origin)
        over = 1 if block == 0 else 0
        for pair_of in range(OWN // 2):
            mixed = []
            for c in (2 * pair_of, 2 * pair_of + 1):
                left = wide_proj[pl.ds(c, RES, stride=2 * OWN), :].astype(BF16)
                right = wide_proj[pl.ds(OWN + c, RES, stride=2 * OWN), :].astype(BF16)
                mixed.append(contract(left, right, over, over).reshape(GROUP, ROWS, RES))
            send_mix[block, :, pair_of] = jnp.concatenate(mixed, axis=1).astype(BF16)

    def gather_mixed(block, copies):
        def take(source, origin):
            values = source[...].astype(F32).reshape(OWN * ROWS, RES)
            wide_mix[pl.ds(pl.multiple_of(origin * OWN * ROWS, OWN * ROWS), OWN * ROWS), :] = values
            return jnp.sum(values.reshape(OWN, ROWS, RES), axis=0)

        total = take(send_mix.at[block, me], me)
        for n, offset in enumerate(OFFSETS):
            copies[n].wait_recv()
            origin = back(offset)
            total = total + take(recv_mix.at[block, origin], origin)
        mean = total * (1.0 / CHANS)
        spread = jnp.zeros_like(mean)
        for part in range(GROUP):
            size = OWN * ROWS
            values = wide_mix[part * size : (part + 1) * size, :].reshape(OWN, ROWS, RES) - mean
            spread = spread + jnp.sum(values * values, axis=0)
        stats[0] = mean
        stats[1] = lax.rsqrt(spread * (1.0 / CHANS) + 1e-05)

    def mid_row(block, i):
        values = wide_mix[pl.ds(i, CHANS, stride=ROWS), :]
        mean, scale = stats[0, i : i + 1, :], stats[1, i : i + 1, :]
        return ((values - mean) * scale * gains[2 + block]).astype(BF16)

    gains[0] = column(norm_gain[0:1, :])
    turn_projection(0)
    for step in range(ROWS // 2):
        turned = [pair[2 * step + h].astype(F32).T for h in range(2)]
        values = jnp.concatenate(turned, axis=1)
        chan_pair[:, step * 256 : (step + 1) * 256] = values
        project(0, step, values)

    pl.semaphore_wait(barrier, len(OFFSETS))
    copies_a = exchange(0, send_proj.at[0], recv_proj.at[0])

    gains[1] = column(norm_gain[1:2, :])
    gains[2] = column(mid_gain[0:1, :])
    gains[3] = column(mid_gain[1:2, :])
    turn_projection(1)
    gate_t[...] = (gate_w[0].astype(F32).T * 0.5).astype(BF16)
    out_t[...] = out_w[0].astype(F32).T.astype(BF16)
    for step in range(ROWS // 2):
        at = slice(step * 256, (step + 1) * 256)
        chan_gate[:, at] = 0.5 * jnp.tanh(contract(gate_t[...], chan_normed[:, at], 1, 0)) + 0.5

    mix(0, copies_a)
    copies_b = exchange(1, send_mix.at[0], recv_mix.at[0])
    gather_mixed(0, copies_b)
    for step in range(ROWS // 2):
        at = slice(step * 256, (step + 1) * 256)
        mid = jnp.concatenate([mid_row(0, 2 * step), mid_row(0, 2 * step + 1)], axis=1)
        update = chan_gate[:, at] * contract(out_t[...], mid, 1, 0)
        values = (chan_pair[:, at] + update).astype(BF16).astype(F32)
        chan_pair[:, at] = values
        project(1, step, values)

    copies_c = exchange(2, send_proj.at[1], recv_proj.at[1])
    half_gate_w = (gate_w[1].astype(F32) * 0.5).astype(BF16)
    for i in range(ROWS):
        at = slice(i * RES, (i + 1) * RES)
        row_gate[i] = 0.5 * jnp.tanh(contract(chan_normed[:, at], half_gate_w, 0, 0)) + 0.5
        row_pair[i] = chan_pair[:, at].T
    mix(1, copies_c)
    copies_d = exchange(3, send_mix.at[1], recv_mix.at[1])
    gather_mixed(1, copies_d)
    for i in range(ROWS):
        update = row_gate[i] * contract(mid_row(1, i), out_w[1], 0, 0)
        result[i] = (row_pair[i] + update).astype(BF16)

    for copies in (copies_a, copies_b, copies_c, copies_d):
        for copy in copies:
            copy.wait_send()


def per_device(pair_rep, proj_weight, gate_weight, out_weight, norm_gain, mid_gain):
    vmem = pl.BlockSpec(memory_space=pltpu.VMEM)
    return pl.pallas_call(
        kernel,
        out_shape=jax.ShapeDtypeStruct((ROWS, RES, CHANS), BF16),
        in_specs=[vmem] * 6,
        out_specs=vmem,
        scratch_shapes=[
            pltpu.VMEM((2, 4, CHANS, CHANS), BF16),
            pltpu.VMEM((CHANS, CHANS), BF16),
            pltpu.VMEM((CHANS, CHANS), BF16),
            pltpu.VMEM((4, CHANS, CHANS), F32),
            pltpu.VMEM((CHANS, ROWS * RES), F32),
            pltpu.VMEM((CHANS, ROWS * RES), BF16),
            pltpu.VMEM((CHANS, ROWS * RES), F32),
            pltpu.VMEM((ROWS, RES, CHANS), F32),
            pltpu.VMEM((ROWS, RES, CHANS), F32),
            pltpu.VMEM((2, GROUP, ROWS, 2 * OWN, RES), BF16),
            pltpu.VMEM((2, GROUP, ROWS, 2 * OWN, RES), BF16),
            pltpu.VMEM((2, GROUP, OWN // 2, 2 * ROWS, RES), BF16),
            pltpu.VMEM((2, GROUP, OWN // 2, 2 * ROWS, RES), BF16),
            pltpu.VMEM((RES * 2 * OWN, RES), F32),
            pltpu.VMEM((CHANS * ROWS, RES), F32),
            pltpu.VMEM((2, ROWS, RES), F32),
            pltpu.SemaphoreType.DMA((4, len(OFFSETS))),
            pltpu.SemaphoreType.DMA((4, len(OFFSETS))),
        ],
        compiler_params=pltpu.CompilerParams(
            collective_id=0, has_side_effects=True, vmem_limit_bytes=32 * 1024 * 1024
        ),
        name="triangles",
    )(pair_rep, proj_weight, gate_weight, out_weight, norm_gain, mid_gain)


def solution(mesh):
    return jax.shard_map(
        per_device,
        mesh=mesh,
        in_specs=(P(("dp", "dap"), None, None), P(), P(), P(), P(), P()),
        out_specs=P(("dp", "dap"), None, None),
        check_vma=False,
    )
```

```python
import jax
import jax.numpy as jnp
from jax import lax
from jax.experimental import pallas as pl
from jax.experimental.pallas import tpu as pltpu
from jax.sharding import PartitionSpec as P

MESH = pl.DeviceIdType.MESH
BF16 = jnp.bfloat16
F32 = jnp.float32
SIDE = 4
GROUP = SIDE * SIDE
RES = 128
CHANS = 128
ROWS = RES // GROUP
OWN = CHANS // GROUP


def far_first(offset):
    return -sum(min(step, SIDE - step) for step in offset)


OFFSETS = sorted(
    [(dy, dx) for dy in range(SIDE) for dx in range(SIDE) if (dy, dx) != (0, 0)], key=far_first
)


def contract(lhs, rhs, lhs_dim, rhs_dim):
    return lax.dot_general(
        lhs, rhs, (((lhs_dim,), (rhs_dim,)), ((), ())), preferred_element_type=F32
    )


def kernel(
    pair_hbm, proj_hbm, gate_hbm, out_hbm, norm_hbm, mid_hbm, result,
    pair, proj_w, gate_w, out_w, norm_gain, mid_gain, load_sem, proj_t, gate_t, out_t, gains, chan_pair, chan_normed, chan_gate, row_gate, row_pair,
    send_proj, recv_proj, send_mix, recv_mix, wide_proj, wide_mix, stats, send_sem, recv_sem,
):
    crop = lax.axis_index("dp")
    me = lax.axis_index("dap")
    y, x = me // SIDE, lax.rem(me, SIDE)

    def towards(offset):
        return lax.rem(y + offset[0], SIDE) * SIDE + lax.rem(x + offset[1], SIDE)

    def back(offset):
        return towards((SIDE - offset[0], SIDE - offset[1]))

    places = (
        (pair_hbm, pair), (proj_hbm, proj_w), (norm_hbm, norm_gain),
        (mid_hbm, mid_gain), (gate_hbm, gate_w), (out_hbm, out_w),
    )
    loads = [pltpu.make_async_copy(*place, load_sem.at[n]) for n, place in enumerate(places)]
    for load in loads:
        load.start()

    barrier = pltpu.get_barrier_semaphore()
    for offset in OFFSETS:
        pl.semaphore_signal(
            barrier, inc=1, device_id=(crop, towards(offset)), device_id_type=MESH
        )

    def exchange(phase, source, target):
        copies = []
        for n, offset in enumerate(OFFSETS):
            there = towards(offset)
            copy = pltpu.make_async_remote_copy(
                src_ref=source.at[there],
                dst_ref=target.at[me],
                send_sem=send_sem.at[phase, n],
                recv_sem=recv_sem.at[phase, n],
                device_id=(crop, there),
                device_id_type=MESH,
            )
            copy.start()
            copies.append(copy)
        return copies

    def column(row):
        return jnp.broadcast_to(row, (CHANS, CHANS)).T

    def turn_projection(block):
        for part in range(4):
            piece = proj_w[block, :, part * CHANS : (part + 1) * CHANS].astype(F32)
            proj_t[block, part] = (piece.T * 0.5).astype(BF16)

    def project(block, step, values):
        mean = jnp.mean(values, axis=0, keepdims=True)
        centered = values - mean
        var = jnp.mean(centered * centered, axis=0, keepdims=True)
        gain = gains[block]
        normed = centered * lax.rsqrt(var + 1e-05) * jnp.concatenate([gain, gain], axis=1)
        normed = normed.astype(BF16)
        chan_normed[:, step * 256 : (step + 1) * 256] = normed
        sides = []
        for side in range(2):
            half_value = contract(proj_t[block, 2 * side], normed, 1, 0)
            half_gate = contract(proj_t[block, 2 * side + 1], normed, 1, 0)
            sides.append(half_value * jnp.tanh(half_gate) + half_value)
        for h in range(2):
            parts = [s[:, h * RES : (h + 1) * RES].reshape(GROUP, OWN, RES) for s in sides]
            send_proj[block, :, 2 * step + h] = jnp.concatenate(parts, axis=1).astype(BF16)

    def widen(block, source, origin):
        wide_proj[pl.ds(pl.multiple_of(origin * RES, RES), RES), :] = (
            source[...].astype(F32).reshape(RES, RES)
        )

    def mix(block, copies):
        widen(block, send_proj.at[block, me], me)
        for n, offset in enumerate(OFFSETS):
            copies[n].wait_recv()
            origin = back(offset)
            widen(block, recv_proj.at[block, origin], origin)
        over = 1 if block == 0 else 0
        for pair_of in range(OWN // 2):
            mixed = []
            for c in (2 * pair_of, 2 * pair_of + 1):
                left = wide_proj[pl.ds(c, RES, stride=2 * OWN), :].astype(BF16)
                right = wide_proj[pl.ds(OWN + c, RES, stride=2 * OWN), :].astype(BF16)
                mixed.append(contract(left, right, over, over).reshape(GROUP, ROWS, RES))
            send_mix[block, :, pair_of] = jnp.concatenate(mixed, axis=1).astype(BF16)

    def gather_mixed(block, copies):
        def take(source, origin):
            values = source[...].astype(F32).reshape(OWN * ROWS, RES)
            wide_mix[pl.ds(pl.multiple_of(origin * OWN * ROWS, OWN * ROWS), OWN * ROWS), :] = values
            return jnp.sum(values.reshape(OWN, ROWS, RES), axis=0)

        total = take(send_mix.at[block, me], me)
        for n, offset in enumerate(OFFSETS):
            copies[n].wait_recv()
            origin = back(offset)
            total = total + take(recv_mix.at[block, origin], origin)
        mean = total * (1.0 / CHANS)
        spread = jnp.zeros_like(mean)
        for part in range(GROUP):
            size = OWN * ROWS
            values = wide_mix[part * size : (part + 1) * size, :].reshape(OWN, ROWS, RES) - mean
            spread = spread + jnp.sum(values * values, axis=0)
        stats[0] = mean
        stats[1] = lax.rsqrt(spread * (1.0 / CHANS) + 1e-05)

    def mid_row(block, i):
        values = wide_mix[pl.ds(i, CHANS, stride=ROWS), :]
        mean, scale = stats[0, i : i + 1, :], stats[1, i : i + 1, :]
        return ((values - mean) * scale * gains[2 + block]).astype(BF16)

    for load in (loads[2], loads[1], loads[0]):
        load.wait()
    gains[0] = column(norm_gain[0:1, :])
    turn_projection(0)
    for step in range(ROWS // 2):
        turned = [pair[2 * step + h].astype(F32).T for h in range(2)]
        values = jnp.concatenate(turned, axis=1)
        chan_pair[:, step * 256 : (step + 1) * 256] = values
        project(0, step, values)

    pl.semaphore_wait(barrier, len(OFFSETS))
    copies_a = exchange(0, send_proj.at[0], recv_proj.at[0])

    for load in loads[3:]:
        load.wait()
    gains[1] = column(norm_gain[1:2, :])
    gains[2] = column(mid_gain[0:1, :])
    gains[3] = column(mid_gain[1:2, :])
    turn_projection(1)
    gate_t[...] = (gate_w[0].astype(F32).T * 0.5).astype(BF16)
    out_t[...] = out_w[0].astype(F32).T.astype(BF16)
    for step in range(ROWS // 2):
        at = slice(step * 256, (step + 1) * 256)
        chan_gate[:, at] = 0.5 * jnp.tanh(contract(gate_t[...], chan_normed[:, at], 1, 0)) + 0.5

    mix(0, copies_a)
    copies_b = exchange(1, send_mix.at[0], recv_mix.at[0])
    gather_mixed(0, copies_b)
    for step in range(ROWS // 2):
        at = slice(step * 256, (step + 1) * 256)
        mid = jnp.concatenate([mid_row(0, 2 * step), mid_row(0, 2 * step + 1)], axis=1)
        update = chan_gate[:, at] * contract(out_t[...], mid, 1, 0)
        values = (chan_pair[:, at] + update).astype(BF16).astype(F32)
        chan_pair[:, at] = values
        project(1, step, values)

    copies_c = exchange(2, send_proj.at[1], recv_proj.at[1])
    half_gate_w = (gate_w[1].astype(F32) * 0.5).astype(BF16)
    for i in range(ROWS):
        at = slice(i * RES, (i + 1) * RES)
        row_gate[i] = 0.5 * jnp.tanh(contract(chan_normed[:, at], half_gate_w, 0, 0)) + 0.5
        row_pair[i] = chan_pair[:, at].T
    mix(1, copies_c)
    copies_d = exchange(3, send_mix.at[1], recv_mix.at[1])
    gather_mixed(1, copies_d)
    for i in range(ROWS):
        update = row_gate[i] * contract(mid_row(1, i), out_w[1], 0, 0)
        result[i] = (row_pair[i] + update).astype(BF16)

    for copies in (copies_a, copies_b, copies_c, copies_d):
        for copy in copies:
            copy.wait_send()


def per_device(pair_rep, proj_weight, gate_weight, out_weight, norm_gain, mid_gain):
    vmem = pl.BlockSpec(memory_space=pltpu.VMEM)
    return pl.pallas_call(
        kernel,
        out_shape=jax.ShapeDtypeStruct((ROWS, RES, CHANS), BF16),
        in_specs=[pl.BlockSpec(memory_space=pltpu.HBM)] * 6,
        out_specs=vmem,
        scratch_shapes=[
            pltpu.VMEM((ROWS, RES, CHANS), BF16),
            pltpu.VMEM((2, CHANS, 4 * CHANS), BF16),
            pltpu.VMEM((2, CHANS, CHANS), BF16),
            pltpu.VMEM((2, CHANS, CHANS), BF16),
            pltpu.VMEM((2, CHANS), F32),
            pltpu.VMEM((2, CHANS), F32),
            pltpu.SemaphoreType.DMA((6,)),
            pltpu.VMEM((2, 4, CHANS, CHANS), BF16),
            pltpu.VMEM((CHANS, CHANS), BF16),
            pltpu.VMEM((CHANS, CHANS), BF16),
            pltpu.VMEM((4, CHANS, CHANS), F32),
            pltpu.VMEM((CHANS, ROWS * RES), F32),
            pltpu.VMEM((CHANS, ROWS * RES), BF16),
            pltpu.VMEM((CHANS, ROWS * RES), F32),
            pltpu.VMEM((ROWS, RES, CHANS), F32),
            pltpu.VMEM((ROWS, RES, CHANS), F32),
            pltpu.VMEM((2, GROUP, ROWS, 2 * OWN, RES), BF16),
            pltpu.VMEM((2, GROUP, ROWS, 2 * OWN, RES), BF16),
            pltpu.VMEM((2, GROUP, OWN // 2, 2 * ROWS, RES), BF16),
            pltpu.VMEM((2, GROUP, OWN // 2, 2 * ROWS, RES), BF16),
            pltpu.VMEM((RES * 2 * OWN, RES), F32),
            pltpu.VMEM((CHANS * ROWS, RES), F32),
            pltpu.VMEM((2, ROWS, RES), F32),
            pltpu.SemaphoreType.DMA((4, len(OFFSETS))),
            pltpu.SemaphoreType.DMA((4, len(OFFSETS))),
        ],
        compiler_params=pltpu.CompilerParams(
            collective_id=0, has_side_effects=True, vmem_limit_bytes=63 * 1024 * 1024
        ),
        name="triangles",
    )(pair_rep, proj_weight, gate_weight, out_weight, norm_gain, mid_gain)


def solution(mesh):
    return jax.shard_map(
        per_device,
        mesh=mesh,
        in_specs=(P(("dp", "dap"), None, None), P(), P(), P(), P(), P()),
        out_specs=P(("dp", "dap"), None, None),
        check_vma=False,
    )
```

```python
import jax
import jax.numpy as jnp
from jax import lax
from jax.experimental import pallas as pl
from jax.experimental.pallas import tpu as pltpu
from jax.sharding import PartitionSpec as P

MESH = pl.DeviceIdType.MESH
BF16 = jnp.bfloat16
F32 = jnp.float32
SIDE = 4
GROUP = SIDE * SIDE
RES = 128
CHANS = 128
ROWS = RES // GROUP
OWN = CHANS // GROUP


def far_first(offset):
    return -sum(min(step, SIDE - step) for step in offset)


OFFSETS = sorted(
    [(dy, dx) for dy in range(SIDE) for dx in range(SIDE) if (dy, dx) != (0, 0)], key=far_first
)


def contract(lhs, rhs, lhs_dim, rhs_dim):
    return lax.dot_general(
        lhs, rhs, (((lhs_dim,), (rhs_dim,)), ((), ())), preferred_element_type=F32
    )


def kernel(
    pair_hbm, proj_hbm, gate_hbm, out_hbm, norm_hbm, mid_hbm, result,
    pair, proj_w, gate_w, out_w, norm_gain, mid_gain, load_sem, proj_t, gate_t, out_t, gains, chan_pair, chan_normed, chan_gate, row_gate, row_pair,
    send_proj, recv_proj, send_mix, recv_mix, wide_proj, wide_mix, stats, send_sem, recv_sem,
):
    crop = lax.axis_index("dp")
    me = lax.axis_index("dap")
    y, x = me // SIDE, lax.rem(me, SIDE)

    def towards(offset):
        return lax.rem(y + offset[0], SIDE) * SIDE + lax.rem(x + offset[1], SIDE)

    places = (
        (pair_hbm, pair), (proj_hbm, proj_w), (norm_hbm, norm_gain),
        (mid_hbm, mid_gain), (gate_hbm, gate_w), (out_hbm, out_w),
    )
    loads = [pltpu.make_async_copy(*place, load_sem.at[n]) for n, place in enumerate(places)]
    for load in loads:
        load.start()

    barrier = pltpu.get_barrier_semaphore()
    for offset in OFFSETS:
        pl.semaphore_signal(
            barrier, inc=1, device_id=(crop, towards(offset)), device_id_type=MESH
        )

    def exchange(phase, source, target):
        for offset in OFFSETS:
            there = towards(offset)
            copy = pltpu.make_async_remote_copy(
                src_ref=source.at[there],
                dst_ref=target.at[me],
                send_sem=send_sem.at[phase],
                recv_sem=recv_sem.at[phase],
                device_id=(crop, there),
                device_id_type=MESH,
            )
            copy.start()
        target[me] = source[me]

    def send_half(half, source, target, sem):
        rows = pl.ds(half * (ROWS // 2), ROWS // 2)
        for offset in OFFSETS:
            there = towards(offset)
            pltpu.make_async_remote_copy(
                src_ref=source.at[there, rows],
                dst_ref=target.at[me, rows],
                send_sem=send_sem.at[sem],
                recv_sem=recv_sem.at[sem],
                device_id=(crop, there),
                device_id_type=MESH,
            ).start()

    def all_of(sem, buffer):
        blocks = buffer.at[pl.ds(0, len(OFFSETS))]
        pltpu.make_async_copy(blocks, blocks, sem).wait()

    def column(row):
        return jnp.broadcast_to(row, (CHANS, CHANS)).T

    def turn_projection(block):
        for part in range(4):
            piece = proj_w[block, :, part * CHANS : (part + 1) * CHANS].astype(F32)
            proj_t[block, part] = (piece.T * 0.5).astype(BF16)

    def project(block, step, values):
        mean = jnp.mean(values, axis=0, keepdims=True)
        centered = values - mean
        var = jnp.mean(centered * centered, axis=0, keepdims=True)
        gain = gains[block]
        normed = centered * lax.rsqrt(var + 1e-05) * jnp.concatenate([gain, gain], axis=1)
        normed = normed.astype(BF16)
        chan_normed[:, step * 256 : (step + 1) * 256] = normed
        sides = []
        for side in range(2):
            half_value = contract(proj_t[block, 2 * side], normed, 1, 0)
            half_gate = contract(proj_t[block, 2 * side + 1], normed, 1, 0)
            sides.append(half_value * jnp.tanh(half_gate) + half_value)
        for h in range(2):
            parts = [s[:, h * RES : (h + 1) * RES].reshape(GROUP, OWN, RES) for s in sides]
            send_proj[block, :, 2 * step + h] = jnp.concatenate(parts, axis=1).astype(BF16)

    def mix(block):
        all_of(recv_sem.at[2 * block], recv_proj.at[block])
        for origin in range(GROUP):
            wide_proj[origin * RES : (origin + 1) * RES, :] = (
                recv_proj[block, origin].astype(F32).reshape(RES, RES)
            )
        over = 1 if block == 0 else 0
        for pair_of in range(OWN // 2):
            mixed = []
            for c in (2 * pair_of, 2 * pair_of + 1):
                left = wide_proj[pl.ds(c, RES, stride=2 * OWN), :].astype(BF16)
                right = wide_proj[pl.ds(OWN + c, RES, stride=2 * OWN), :].astype(BF16)
                mixed.append(contract(left, right, over, over).reshape(GROUP, ROWS, RES))
            send_mix[block, :, pair_of] = jnp.concatenate(mixed, axis=1).astype(BF16)

    def gather_mixed(block):
        all_of(recv_sem.at[2 * block + 1], recv_mix.at[block])
        size = OWN * ROWS
        total = jnp.zeros((ROWS, RES), F32)
        for origin in range(GROUP):
            values = recv_mix[block, origin].astype(F32).reshape(size, RES)
            wide_mix[origin * size : (origin + 1) * size, :] = values
            total = total + jnp.sum(values.reshape(OWN, ROWS, RES), axis=0)
        mean = total * (1.0 / CHANS)
        spread = jnp.zeros_like(mean)
        for origin in range(GROUP):
            values = wide_mix[origin * size : (origin + 1) * size, :].reshape(OWN, ROWS, RES) - mean
            spread = spread + jnp.sum(values * values, axis=0)
        stats[0] = mean
        stats[1] = lax.rsqrt(spread * (1.0 / CHANS) + 1e-05)

    def mid_row(block, i):
        values = wide_mix[pl.ds(i, CHANS, stride=ROWS), :]
        mean, scale = stats[0, i : i + 1, :], stats[1, i : i + 1, :]
        return ((values - mean) * scale * gains[2 + block]).astype(BF16)

    for load in (loads[2], loads[1], loads[0]):
        load.wait()
    gains[0] = column(norm_gain[0:1, :])
    turn_projection(0)
    for step in range(ROWS // 2):
        turned = [pair[2 * step + h].astype(F32).T for h in range(2)]
        values = jnp.concatenate(turned, axis=1)
        chan_pair[:, step * 256 : (step + 1) * 256] = values
        project(0, step, values)

    pl.semaphore_wait(barrier, len(OFFSETS))
    exchange(0, send_proj.at[0], recv_proj.at[0])

    for load in loads[3:]:
        load.wait()
    gains[1] = column(norm_gain[1:2, :])
    gains[2] = column(mid_gain[0:1, :])
    gains[3] = column(mid_gain[1:2, :])
    turn_projection(1)
    gate_t[...] = (gate_w[0].astype(F32).T * 0.5).astype(BF16)
    out_t[...] = out_w[0].astype(F32).T.astype(BF16)
    for step in range(ROWS // 2):
        at = slice(step * 256, (step + 1) * 256)
        chan_gate[:, at] = 0.5 * jnp.tanh(contract(gate_t[...], chan_normed[:, at], 1, 0)) + 0.5

    mix(0)
    exchange(1, send_mix.at[0], recv_mix.at[0])
    gather_mixed(0)
    for step in range(ROWS // 2):
        at = slice(step * 256, (step + 1) * 256)
        mid = jnp.concatenate([mid_row(0, 2 * step), mid_row(0, 2 * step + 1)], axis=1)
        update = chan_gate[:, at] * contract(out_t[...], mid, 1, 0)
        values = (chan_pair[:, at] + update).astype(BF16).astype(F32)
        chan_pair[:, at] = values
        project(1, step, values)
        if step % 2 == 1:
            send_half(step // 2, send_proj.at[1], recv_proj.at[1], 2)

    recv_proj[1, me] = send_proj[1, me]
    half_gate_w = (gate_w[1].astype(F32) * 0.5).astype(BF16)
    for i in range(ROWS):
        at = slice(i * RES, (i + 1) * RES)
        row_gate[i] = 0.5 * jnp.tanh(contract(chan_normed[:, at], half_gate_w, 0, 0)) + 0.5
        row_pair[i] = chan_pair[:, at].T
    mix(1)
    exchange(3, send_mix.at[1], recv_mix.at[1])
    gather_mixed(1)
    for i in range(ROWS):
        update = row_gate[i] * contract(mid_row(1, i), out_w[1], 0, 0)
        result[i] = (row_pair[i] + update).astype(BF16)

    for block in range(2):
        all_of(send_sem.at[2 * block], send_proj.at[block])
        all_of(send_sem.at[2 * block + 1], send_mix.at[block])


def per_device(pair_rep, proj_weight, gate_weight, out_weight, norm_gain, mid_gain):
    operands = (pair_rep, proj_weight, gate_weight, out_weight, norm_gain, mid_gain)
    operands = [pltpu.with_memory_space_constraint(value, pltpu.HBM) for value in operands]
    return pl.pallas_call(
        kernel,
        out_shape=jax.ShapeDtypeStruct((ROWS, RES, CHANS), BF16),
        in_specs=[pl.BlockSpec(memory_space=pltpu.HBM)] * 6,
        out_specs=pl.BlockSpec(memory_space=pltpu.VMEM),
        scratch_shapes=[
            pltpu.VMEM((ROWS, RES, CHANS), BF16),
            pltpu.VMEM((2, CHANS, 4 * CHANS), BF16),
            pltpu.VMEM((2, CHANS, CHANS), BF16),
            pltpu.VMEM((2, CHANS, CHANS), BF16),
            pltpu.VMEM((2, CHANS), F32),
            pltpu.VMEM((2, CHANS), F32),
            pltpu.SemaphoreType.DMA((6,)),
            pltpu.VMEM((2, 4, CHANS, CHANS), BF16),
            pltpu.VMEM((CHANS, CHANS), BF16),
            pltpu.VMEM((CHANS, CHANS), BF16),
            pltpu.VMEM((4, CHANS, CHANS), F32),
            pltpu.VMEM((CHANS, ROWS * RES), F32),
            pltpu.VMEM((CHANS, ROWS * RES), BF16),
            pltpu.VMEM((CHANS, ROWS * RES), F32),
            pltpu.VMEM((ROWS, RES, CHANS), F32),
            pltpu.VMEM((ROWS, RES, CHANS), F32),
            pltpu.VMEM((2, GROUP, ROWS, 2 * OWN, RES), BF16),
            pltpu.VMEM((2, GROUP, ROWS, 2 * OWN, RES), BF16),
            pltpu.VMEM((2, GROUP, OWN // 2, 2 * ROWS, RES), BF16),
            pltpu.VMEM((2, GROUP, OWN // 2, 2 * ROWS, RES), BF16),
            pltpu.VMEM((RES * 2 * OWN, RES), F32),
            pltpu.VMEM((CHANS * ROWS, RES), F32),
            pltpu.VMEM((2, ROWS, RES), F32),
            pltpu.SemaphoreType.DMA((4,)),
            pltpu.SemaphoreType.DMA((4,)),
        ],
        compiler_params=pltpu.CompilerParams(
            collective_id=0, has_side_effects=True, vmem_limit_bytes=32 * 1024 * 1024
        ),
        name="triangles",
    )(*operands)


def solution(mesh):
    return jax.shard_map(
        per_device,
        mesh=mesh,
        in_specs=(P(("dp", "dap"), None, None), P(), P(), P(), P(), P()),
        out_specs=P(("dp", "dap"), None, None),
        check_vma=False,
    )
```

```python
import jax
import jax.numpy as jnp
from jax import lax
from jax.experimental import pallas as pl
from jax.experimental.pallas import tpu as pltpu
from jax.sharding import PartitionSpec as P

MESH = pl.DeviceIdType.MESH
BF16 = jnp.bfloat16
F32 = jnp.float32
SIDE = 4
GROUP = SIDE * SIDE
RES = 128
CHANS = 128
ROWS = RES // GROUP
OWN = CHANS // GROUP
PART = OWN // 2
STEPS = ROWS // 2


def far_first(offset):
    return -sum(min(step, SIDE - step) for step in offset)


OFFSETS = sorted(
    [(dy, dx) for dy in range(SIDE) for dx in range(SIDE) if (dy, dx) != (0, 0)], key=far_first
)

PLAN = {1: ((0, 0, 2), (1, 0, 2)), 3: ((0, 2, 2), (1, 2, 2))}


def contract(lhs, rhs, lhs_dim, rhs_dim):
    return lax.dot_general(
        lhs, rhs, (((lhs_dim,), (rhs_dim,)), ((), ())), preferred_element_type=F32
    )


def kernel(
    pair_hbm, proj_hbm, gate_hbm, out_hbm, norm_hbm, mid_hbm, result,
    pair, proj_w, gate_w, out_w, norm_gain, mid_gain, load_sem, turned, proj_t, gate_t, out_t, gains, chan_pair, chan_normed, chan_gate, row_gate, row_pair,
    send_proj, recv_proj, send_mix, recv_mix, wide_proj, wide_mix, stats, send_sem, recv_sem,
):
    crop = lax.axis_index("dp")
    me = lax.axis_index("dap")
    y, x = me // SIDE, lax.rem(me, SIDE)

    def towards(offset):
        return lax.rem(y + offset[0], SIDE) * SIDE + lax.rem(x + offset[1], SIDE)

    places = (
        (proj_hbm, proj_w), (norm_hbm, norm_gain), (mid_hbm, mid_gain),
        (gate_hbm, gate_w), (out_hbm, out_w),
    )
    loads = [pltpu.make_async_copy(*place, load_sem.at[n]) for n, place in enumerate(places)]
    for step in range(STEPS):
        rows = pl.ds(2 * step, 2)
        loads.append(
            pltpu.make_async_copy(pair_hbm.at[rows], pair.at[rows], load_sem.at[5 + step])
        )
    for load in loads:
        load.start()

    barrier = pltpu.get_barrier_semaphore()
    for offset in OFFSETS:
        pl.semaphore_signal(
            barrier, inc=1, device_id=(crop, towards(offset)), device_id_type=MESH
        )

    def exchange(sem, source, target, cut=None):
        for offset in OFFSETS:
            there = towards(offset)
            from_ref, to_ref = source.at[there], target.at[me]
            if cut is not None:
                from_ref, to_ref = from_ref.at[pl.ds(*cut)], to_ref.at[pl.ds(*cut)]
            pltpu.make_async_remote_copy(
                src_ref=from_ref,
                dst_ref=to_ref,
                send_sem=send_sem.at[sem],
                recv_sem=recv_sem.at[sem],
                device_id=(crop, there),
                device_id_type=MESH,
            ).start()

    def exchange_projected(block, step):
        for part, *cut in PLAN.get(step, ()):
            exchange(4 * block + part, send_proj.at[block, part], recv_proj.at[block, part], cut)

    def all_of(sem, buffer):
        blocks = buffer.at[pl.ds(0, len(OFFSETS))]
        pltpu.make_async_copy(blocks, blocks, sem).wait()

    def column(row):
        return jnp.broadcast_to(row, (CHANS, CHANS)).T

    def turn_projection(block):
        for half in range(4):
            side, kind = half // 2, half % 2
            piece = proj_w[block, :, half * CHANS : (half + 1) * CHANS].astype(F32).T * 0.5
            for n in range(CHANS // PART):
                at = (2 * n + side) * PART
                turned[kind, at : at + PART, :] = piece[n * PART : (n + 1) * PART, :]
        for kind in range(2):
            proj_t[block, kind] = turned[kind].astype(BF16)

    def project(block, step, values):
        mean = jnp.mean(values, axis=0, keepdims=True)
        centered = values - mean
        var = jnp.mean(centered * centered, axis=0, keepdims=True)
        gain = gains[block]
        normed = centered * lax.rsqrt(var + 1e-05) * jnp.concatenate([gain, gain], axis=1)
        normed = normed.astype(BF16)
        chan_normed[:, step * 256 : (step + 1) * 256] = normed
        for half in range(2):
            at = slice(half * CHANS, (half + 1) * CHANS)
            half_value = contract(proj_t[block, 0, at], normed, 1, 0)
            half_gate = contract(proj_t[block, 1, at], normed, 1, 0)
            sides = half_value * jnp.tanh(half_gate) + half_value
            rows = [
                sides[:, h * RES : (h + 1) * RES].reshape(GROUP // 2, 2, 2 * PART, RES)
                for h in range(2)
            ]
            both = jnp.concatenate(rows, axis=2).astype(BF16)
            owners = slice(half * GROUP // 2, (half + 1) * GROUP // 2)
            for part in range(2):
                send_proj[block, part, owners, step] = both[:, part]

    def keep_own(sent, received):
        received[me] = sent[me]

    def mix(block):
        over = 1 if block == 0 else 0
        size = 2 * PART * ROWS
        for part in range(2):
            all_of(recv_sem.at[4 * block + part], recv_proj.at[block, part])
            for origin in range(GROUP):
                wide_proj[part, origin * size : (origin + 1) * size, :] = (
                    recv_proj[block, part, origin].astype(F32).reshape(size, RES)
                )
            for pair_of in range(PART // 2):
                mixed = []
                for c in (2 * pair_of, 2 * pair_of + 1):
                    left = wide_proj[part, pl.ds(c, RES, stride=2 * PART), :].astype(BF16)
                    right = wide_proj[part, pl.ds(PART + c, RES, stride=2 * PART), :].astype(BF16)
                    mixed.append(contract(left, right, over, over).reshape(GROUP, ROWS, RES))
                send_mix[block, part, :, pair_of] = jnp.concatenate(mixed, axis=1).astype(BF16)
            exchange(4 * block + 2 + part, send_mix.at[block, part], recv_mix.at[block, part])
            keep_own(send_mix.at[block, part], recv_mix.at[block, part])

    def gather_mixed(block):
        size = OWN * ROWS
        total = jnp.zeros((ROWS, RES), F32)
        for part in range(2):
            all_of(recv_sem.at[4 * block + 2 + part], recv_mix.at[block, part])
            for origin in range(GROUP):
                values = recv_mix[block, part, origin].astype(F32).reshape(PART * ROWS, RES)
                at = origin * size + part * PART * ROWS
                wide_mix[at : at + PART * ROWS, :] = values
                total = total + jnp.sum(values.reshape(PART, ROWS, RES), axis=0)
        mean = total * (1.0 / CHANS)
        spread = jnp.zeros_like(mean)
        for origin in range(GROUP):
            values = wide_mix[origin * size : (origin + 1) * size, :].reshape(OWN, ROWS, RES) - mean
            spread = spread + jnp.sum(values * values, axis=0)
        stats[0] = mean
        stats[1] = lax.rsqrt(spread * (1.0 / CHANS) + 1e-05)

    def mid_row(block, i):
        values = wide_mix[pl.ds(i, CHANS, stride=ROWS), :]
        mean, scale = stats[0, i : i + 1, :], stats[1, i : i + 1, :]
        return ((values - mean) * scale * gains[2 + block]).astype(BF16)

    loads[1].wait()
    loads[0].wait()
    gains[0] = column(norm_gain[0:1, :])
    turn_projection(0)
    for step in range(STEPS):
        loads[5 + step].wait()
        values = jnp.concatenate([pair[2 * step + h].astype(F32).T for h in range(2)], axis=1)
        chan_pair[:, step * 256 : (step + 1) * 256] = values
        project(0, step, values)
        if step == min(PLAN):
            pl.semaphore_wait(barrier, len(OFFSETS))
        exchange_projected(0, step)
    for part in range(2):
        keep_own(send_proj.at[0, part], recv_proj.at[0, part])

    for load in loads[2:5]:
        load.wait()
    gains[1] = column(norm_gain[1:2, :])
    gains[2] = column(mid_gain[0:1, :])
    gains[3] = column(mid_gain[1:2, :])
    turn_projection(1)
    gate_t[...] = (gate_w[0].astype(F32).T * 0.5).astype(BF16)
    out_t[...] = out_w[0].astype(F32).T.astype(BF16)
    for step in range(STEPS):
        at = slice(step * 256, (step + 1) * 256)
        chan_gate[:, at] = 0.5 * jnp.tanh(contract(gate_t[...], chan_normed[:, at], 1, 0)) + 0.5

    mix(0)
    gather_mixed(0)
    for step in range(STEPS):
        at = slice(step * 256, (step + 1) * 256)
        mid = jnp.concatenate([mid_row(0, 2 * step), mid_row(0, 2 * step + 1)], axis=1)
        update = chan_gate[:, at] * contract(out_t[...], mid, 1, 0)
        values = (chan_pair[:, at] + update).astype(BF16).astype(F32)
        chan_pair[:, at] = values
        project(1, step, values)
        exchange_projected(1, step)

    for part in range(2):
        keep_own(send_proj.at[1, part], recv_proj.at[1, part])
    half_gate_w = (gate_w[1].astype(F32) * 0.5).astype(BF16)
    for i in range(ROWS):
        at = slice(i * RES, (i + 1) * RES)
        row_gate[i] = 0.5 * jnp.tanh(contract(chan_normed[:, at], half_gate_w, 0, 0)) + 0.5
        row_pair[i] = chan_pair[:, at].T
    mix(1)
    gather_mixed(1)
    for i in range(ROWS):
        update = row_gate[i] * contract(mid_row(1, i), out_w[1], 0, 0)
        result[i] = (row_pair[i] + update).astype(BF16)

    for block in range(2):
        for part in range(2):
            all_of(send_sem.at[4 * block + part], send_proj.at[block, part])
            all_of(send_sem.at[4 * block + 2 + part], send_mix.at[block, part])


def per_device(pair_rep, proj_weight, gate_weight, out_weight, norm_gain, mid_gain):
    operands = (pair_rep, proj_weight, gate_weight, out_weight, norm_gain, mid_gain)
    operands = [pltpu.with_memory_space_constraint(value, pltpu.HBM) for value in operands]
    return pl.pallas_call(
        kernel,
        out_shape=jax.ShapeDtypeStruct((ROWS, RES, CHANS), BF16),
        in_specs=[pl.BlockSpec(memory_space=pltpu.HBM)] * 6,
        out_specs=pl.BlockSpec(memory_space=pltpu.VMEM),
        scratch_shapes=[
            pltpu.VMEM((ROWS, RES, CHANS), BF16),
            pltpu.VMEM((2, CHANS, 4 * CHANS), BF16),
            pltpu.VMEM((2, CHANS, CHANS), BF16),
            pltpu.VMEM((2, CHANS, CHANS), BF16),
            pltpu.VMEM((2, CHANS), F32),
            pltpu.VMEM((2, CHANS), F32),
            pltpu.SemaphoreType.DMA((5 + STEPS,)),
            pltpu.VMEM((2, 2 * CHANS, CHANS), F32),
            pltpu.VMEM((2, 2, 2 * CHANS, CHANS), BF16),
            pltpu.VMEM((CHANS, CHANS), BF16),
            pltpu.VMEM((CHANS, CHANS), BF16),
            pltpu.VMEM((4, CHANS, CHANS), F32),
            pltpu.VMEM((CHANS, ROWS * RES), F32),
            pltpu.VMEM((CHANS, ROWS * RES), BF16),
            pltpu.VMEM((CHANS, ROWS * RES), F32),
            pltpu.VMEM((ROWS, RES, CHANS), F32),
            pltpu.VMEM((ROWS, RES, CHANS), F32),
            pltpu.VMEM((2, 2, GROUP, STEPS, 4 * PART, RES), BF16),
            pltpu.VMEM((2, 2, GROUP, STEPS, 4 * PART, RES), BF16),
            pltpu.VMEM((2, 2, GROUP, PART // 2, 2 * ROWS, RES), BF16),
            pltpu.VMEM((2, 2, GROUP, PART // 2, 2 * ROWS, RES), BF16),
            pltpu.VMEM((2, RES * 2 * PART, RES), F32),
            pltpu.VMEM((CHANS * ROWS, RES), F32),
            pltpu.VMEM((2, ROWS, RES), F32),
            pltpu.SemaphoreType.DMA((8,)),
            pltpu.SemaphoreType.DMA((8,)),
        ],
        compiler_params=pltpu.CompilerParams(
            collective_id=0, has_side_effects=True, vmem_limit_bytes=32 * 1024 * 1024
        ),
        name="triangles",
    )(*operands)


def solution(mesh):
    return jax.shard_map(
        per_device,
        mesh=mesh,
        in_specs=(P(("dp", "dap"), None, None), P(), P(), P(), P(), P()),
        out_specs=P(("dp", "dap"), None, None),
        check_vma=False,
    )
```

```python
import jax
import jax.numpy as jnp
from jax import lax
from jax.experimental import pallas as pl
from jax.experimental.pallas import tpu as pltpu
from jax.sharding import PartitionSpec as P

MESH = pl.DeviceIdType.MESH
BF16 = jnp.bfloat16
F32 = jnp.float32
SIDE = 4
GROUP = SIDE * SIDE
RES = 128
CHANS = 128
ROWS = RES // GROUP
OWN = CHANS // GROUP
PART = OWN // 2
STEPS = ROWS // 2


def far_first(offset):
    return -sum(min(step, SIDE - step) for step in offset)


OFFSETS = sorted(
    [(dy, dx) for dy in range(SIDE) for dx in range(SIDE) if (dy, dx) != (0, 0)], key=far_first
)

PLAN = {1: ((0, 0, 2), (1, 0, 2)), 3: ((0, 2, 2), (1, 2, 2))}


def contract(lhs, rhs, lhs_dim, rhs_dim):
    return lax.dot_general(
        lhs, rhs, (((lhs_dim,), (rhs_dim,)), ((), ())), preferred_element_type=F32
    )


def kernel(
    pair_hbm, proj_hbm, gate_hbm, out_hbm, norm_hbm, mid_hbm, result,
    pair, proj_w, gate_w, out_w, norm_gain, mid_gain, load_sem, turned, proj_t, gate_t, out_t, gains, chan_pair, chan_normed, chan_gate, row_gate, row_pair,
    send_proj, recv_proj, send_mix, recv_mix, wide_proj, wide_mix, stats, send_sem, recv_sem, entered,
):
    crop = lax.axis_index("dp")
    me = lax.axis_index("dap")
    y, x = me // SIDE, lax.rem(me, SIDE)

    def towards(offset):
        return lax.rem(y + offset[0], SIDE) * SIDE + lax.rem(x + offset[1], SIDE)

    places = (
        (proj_hbm, proj_w), (norm_hbm, norm_gain), (mid_hbm, mid_gain),
        (gate_hbm, gate_w), (out_hbm, out_w),
    )
    loads = [pltpu.make_async_copy(*place, load_sem.at[n]) for n, place in enumerate(places)]
    for step in range(STEPS):
        rows = pl.ds(2 * step, 2)
        loads.append(
            pltpu.make_async_copy(pair_hbm.at[rows], pair.at[rows], load_sem.at[5 + step])
        )
    for load in loads[:2] + loads[5:]:
        load.start()

    barrier = pltpu.get_barrier_semaphore()

    @pl.when(me != 0)
    def _():
        for offset in OFFSETS:
            pl.semaphore_signal(
                barrier, inc=1, device_id=(crop, towards(offset)), device_id_type=MESH
            )

    @pl.when(me == 0)
    def _():
        pl.semaphore_wait(barrier, len(OFFSETS))
        for offset in OFFSETS:
            pl.semaphore_signal(
                entered, inc=1, device_id=(crop, towards(offset)), device_id_type=MESH
            )

    for load in loads[2:5]:
        load.start()

    def send_to(there, sem, source, target, cut=None):
        from_ref, to_ref = source.at[there], target.at[me]
        if cut is not None:
            from_ref, to_ref = from_ref.at[pl.ds(*cut)], to_ref.at[pl.ds(*cut)]
        pltpu.make_async_remote_copy(
            src_ref=from_ref,
            dst_ref=to_ref,
            send_sem=send_sem.at[sem],
            recv_sem=recv_sem.at[sem],
            device_id=(crop, there),
            device_id_type=MESH,
        ).start()

    def exchange(sem, source, target, cut=None):
        for offset in OFFSETS:
            send_to(towards(offset), sem, source, target, cut)

    def send_first(step):
        for part, *cut in PLAN.get(step, ()):
            for offset in OFFSETS:
                there = towards(offset)

                @pl.when(there != 0)
                def _():
                    send_to(there, part, send_proj.at[0, part], recv_proj.at[0, part], cut)

    def send_second(step):
        for part, *cut in PLAN.get(step, ()):
            exchange(4 + part, send_proj.at[1, part], recv_proj.at[1, part], cut)

    def all_of(sem, buffer):
        blocks = buffer.at[pl.ds(0, len(OFFSETS))]
        pltpu.make_async_copy(blocks, blocks, sem).wait()

    def column(row):
        return jnp.broadcast_to(row, (CHANS, CHANS)).T

    def turn_projection(block):
        for half in range(4):
            side, kind = half // 2, half % 2
            piece = proj_w[block, :, half * CHANS : (half + 1) * CHANS].astype(F32).T * 0.5
            for n in range(CHANS // PART):
                at = (2 * n + side) * PART
                turned[kind, at : at + PART, :] = piece[n * PART : (n + 1) * PART, :]
        for kind in range(2):
            proj_t[block, kind] = turned[kind].astype(BF16)

    def project(block, step, values):
        mean = jnp.mean(values, axis=0, keepdims=True)
        centered = values - mean
        var = jnp.mean(centered * centered, axis=0, keepdims=True)
        gain = gains[block]
        normed = centered * lax.rsqrt(var + 1e-05) * jnp.concatenate([gain, gain], axis=1)
        normed = normed.astype(BF16)
        chan_normed[:, step * 256 : (step + 1) * 256] = normed
        for half in range(2):
            at = slice(half * CHANS, (half + 1) * CHANS)
            half_value = contract(proj_t[block, 0, at], normed, 1, 0)
            half_gate = contract(proj_t[block, 1, at], normed, 1, 0)
            sides = half_value * jnp.tanh(half_gate) + half_value
            rows = [
                sides[:, h * RES : (h + 1) * RES].reshape(GROUP // 2, 2, 2 * PART, RES)
                for h in range(2)
            ]
            both = jnp.concatenate(rows, axis=2).astype(BF16)
            owners = slice(half * GROUP // 2, (half + 1) * GROUP // 2)
            for part in range(2):
                send_proj[block, part, owners, step] = both[:, part]

    def keep_own(sent, received):
        received[me] = sent[me]

    def mix(block):
        over = 1 if block == 0 else 0
        size = 2 * PART * ROWS
        for part in range(2):
            all_of(recv_sem.at[4 * block + part], recv_proj.at[block, part])
            for origin in range(GROUP):
                wide_proj[part, origin * size : (origin + 1) * size, :] = (
                    recv_proj[block, part, origin].astype(F32).reshape(size, RES)
                )
            for pair_of in range(PART // 2):
                mixed = []
                for c in (2 * pair_of, 2 * pair_of + 1):
                    left = wide_proj[part, pl.ds(c, RES, stride=2 * PART), :].astype(BF16)
                    right = wide_proj[part, pl.ds(PART + c, RES, stride=2 * PART), :].astype(BF16)
                    mixed.append(contract(left, right, over, over).reshape(GROUP, ROWS, RES))
                send_mix[block, part, :, pair_of] = jnp.concatenate(mixed, axis=1).astype(BF16)
            exchange(4 * block + 2 + part, send_mix.at[block, part], recv_mix.at[block, part])
            keep_own(send_mix.at[block, part], recv_mix.at[block, part])

    def gather_mixed(block):
        size = OWN * ROWS
        total = jnp.zeros((ROWS, RES), F32)
        for part in range(2):
            all_of(recv_sem.at[4 * block + 2 + part], recv_mix.at[block, part])
            for origin in range(GROUP):
                values = recv_mix[block, part, origin].astype(F32).reshape(PART * ROWS, RES)
                at = origin * size + part * PART * ROWS
                wide_mix[at : at + PART * ROWS, :] = values
                total = total + jnp.sum(values.reshape(PART, ROWS, RES), axis=0)
        mean = total * (1.0 / CHANS)
        spread = jnp.zeros_like(mean)
        for origin in range(GROUP):
            values = wide_mix[origin * size : (origin + 1) * size, :].reshape(OWN, ROWS, RES) - mean
            spread = spread + jnp.sum(values * values, axis=0)
        stats[0] = mean
        stats[1] = lax.rsqrt(spread * (1.0 / CHANS) + 1e-05)

    def mid_row(block, i):
        values = wide_mix[pl.ds(i, CHANS, stride=ROWS), :]
        mean, scale = stats[0, i : i + 1, :], stats[1, i : i + 1, :]
        return ((values - mean) * scale * gains[2 + block]).astype(BF16)

    loads[1].wait()
    loads[0].wait()
    gains[0] = column(norm_gain[0:1, :])
    turn_projection(0)
    for step in range(STEPS):
        loads[5 + step].wait()
        values = jnp.concatenate([pair[2 * step + h].astype(F32).T for h in range(2)], axis=1)
        chan_pair[:, step * 256 : (step + 1) * 256] = values
        project(0, step, values)
        if step == min(PLAN):

            @pl.when(me != 0)
            def _():
                pl.semaphore_wait(barrier, len(OFFSETS) - 1)

        send_first(step)

    @pl.when(me != 0)
    def _():
        pl.semaphore_wait(entered, 1)
        for part in range(2):
            send_to(0, part, send_proj.at[0, part], recv_proj.at[0, part])

    for part in range(2):
        keep_own(send_proj.at[0, part], recv_proj.at[0, part])

    for load in loads[2:5]:
        load.wait()
    gains[1] = column(norm_gain[1:2, :])
    gains[2] = column(mid_gain[0:1, :])
    gains[3] = column(mid_gain[1:2, :])
    turn_projection(1)
    gate_t[...] = (gate_w[0].astype(F32).T * 0.5).astype(BF16)
    out_t[...] = out_w[0].astype(F32).T.astype(BF16)
    for step in range(STEPS):
        at = slice(step * 256, (step + 1) * 256)
        chan_gate[:, at] = 0.5 * jnp.tanh(contract(gate_t[...], chan_normed[:, at], 1, 0)) + 0.5

    mix(0)
    gather_mixed(0)
    for step in range(STEPS):
        at = slice(step * 256, (step + 1) * 256)
        mid = jnp.concatenate([mid_row(0, 2 * step), mid_row(0, 2 * step + 1)], axis=1)
        update = chan_gate[:, at] * contract(out_t[...], mid, 1, 0)
        values = (chan_pair[:, at] + update).astype(BF16).astype(F32)
        chan_pair[:, at] = values
        project(1, step, values)
        send_second(step)

    for part in range(2):
        keep_own(send_proj.at[1, part], recv_proj.at[1, part])
    half_gate_w = (gate_w[1].astype(F32) * 0.5).astype(BF16)
    for i in range(ROWS):
        at = slice(i * RES, (i + 1) * RES)
        row_gate[i] = 0.5 * jnp.tanh(contract(chan_normed[:, at], half_gate_w, 0, 0)) + 0.5
        row_pair[i] = chan_pair[:, at].T
    mix(1)
    gather_mixed(1)
    for i in range(ROWS):
        update = row_gate[i] * contract(mid_row(1, i), out_w[1], 0, 0)
        result[i] = (row_pair[i] + update).astype(BF16)

    for block in range(2):
        for part in range(2):
            all_of(send_sem.at[4 * block + part], send_proj.at[block, part])
            all_of(send_sem.at[4 * block + 2 + part], send_mix.at[block, part])


def per_device(pair_rep, proj_weight, gate_weight, out_weight, norm_gain, mid_gain):
    operands = (pair_rep, proj_weight, gate_weight, out_weight, norm_gain, mid_gain)
    operands = [pltpu.with_memory_space_constraint(value, pltpu.HBM) for value in operands]
    return pl.pallas_call(
        kernel,
        out_shape=jax.ShapeDtypeStruct((ROWS, RES, CHANS), BF16),
        in_specs=[pl.BlockSpec(memory_space=pltpu.HBM)] * 6,
        out_specs=pl.BlockSpec(memory_space=pltpu.VMEM),
        scratch_shapes=[
            pltpu.VMEM((ROWS, RES, CHANS), BF16),
            pltpu.VMEM((2, CHANS, 4 * CHANS), BF16),
            pltpu.VMEM((2, CHANS, CHANS), BF16),
            pltpu.VMEM((2, CHANS, CHANS), BF16),
            pltpu.VMEM((2, CHANS), F32),
            pltpu.VMEM((2, CHANS), F32),
            pltpu.SemaphoreType.DMA((5 + STEPS,)),
            pltpu.VMEM((2, 2 * CHANS, CHANS), F32),
            pltpu.VMEM((2, 2, 2 * CHANS, CHANS), BF16),
            pltpu.VMEM((CHANS, CHANS), BF16),
            pltpu.VMEM((CHANS, CHANS), BF16),
            pltpu.VMEM((4, CHANS, CHANS), F32),
            pltpu.VMEM((CHANS, ROWS * RES), F32),
            pltpu.VMEM((CHANS, ROWS * RES), BF16),
            pltpu.VMEM((CHANS, ROWS * RES), F32),
            pltpu.VMEM((ROWS, RES, CHANS), F32),
            pltpu.VMEM((ROWS, RES, CHANS), F32),
            pltpu.VMEM((2, 2, GROUP, STEPS, 4 * PART, RES), BF16),
            pltpu.VMEM((2, 2, GROUP, STEPS, 4 * PART, RES), BF16),
            pltpu.VMEM((2, 2, GROUP, PART // 2, 2 * ROWS, RES), BF16),
            pltpu.VMEM((2, 2, GROUP, PART // 2, 2 * ROWS, RES), BF16),
            pltpu.VMEM((2, RES * 2 * PART, RES), F32),
            pltpu.VMEM((CHANS * ROWS, RES), F32),
            pltpu.VMEM((2, ROWS, RES), F32),
            pltpu.SemaphoreType.DMA((8,)),
            pltpu.SemaphoreType.DMA((8,)),
            pltpu.SemaphoreType.REGULAR,
        ],
        compiler_params=pltpu.CompilerParams(
            collective_id=0, has_side_effects=True, vmem_limit_bytes=32 * 1024 * 1024
        ),
        name="triangles",
    )(*operands)


def solution(mesh):
    return jax.shard_map(
        per_device,
        mesh=mesh,
        in_specs=(P(("dp", "dap"), None, None), P(), P(), P(), P(), P()),
        out_specs=P(("dp", "dap"), None, None),
        check_vma=False,
    )
```

```python
import jax
import jax.numpy as jnp
from jax import lax
from jax.experimental import pallas as pl
from jax.experimental.pallas import tpu as pltpu
from jax.sharding import PartitionSpec as P

MESH = pl.DeviceIdType.MESH
BF16 = jnp.bfloat16
F32 = jnp.float32
SIDE = 4
GROUP = SIDE * SIDE
RES = 128
CHANS = 128
ROWS = RES // GROUP
OWN = CHANS // GROUP
PART = OWN // 2
STEPS = ROWS // 2


def far_first(offset):
    return -sum(min(step, SIDE - step) for step in offset)


OFFSETS = sorted(
    [(dy, dx) for dy in range(SIDE) for dx in range(SIDE) if (dy, dx) != (0, 0)], key=far_first
)

PLAN = (
    {1: ((0, 0, 2), (1, 0, 2)), 3: ((0, 2, 2), (1, 2, 2))},
    {1: ((0, 0, 2),), 3: ((0, 2, 2), (1, 0, 4))},
)


def contract(lhs, rhs, lhs_dim, rhs_dim):
    return lax.dot_general(
        lhs, rhs, (((lhs_dim,), (rhs_dim,)), ((), ())), preferred_element_type=F32
    )


def kernel(
    pair_hbm, proj_hbm, gate_hbm, out_hbm, norm_hbm, mid_hbm, result,
    pair, proj_w, gate_w, out_w, norm_gain, mid_gain, load_sem, picks, proj_t, gate_t, out_t, gains, chan_pair, chan_normed, chan_gate, row_gate, row_pair,
    send_proj, recv_proj, send_mix, recv_mix, wide_proj, wide_mix, stats, send_sem, recv_sem, entered,
):
    crop = lax.axis_index("dp")
    me = lax.axis_index("dap")
    y, x = me // SIDE, lax.rem(me, SIDE)

    def towards(offset):
        return lax.rem(y + offset[0], SIDE) * SIDE + lax.rem(x + offset[1], SIDE)

    places = (
        (proj_hbm, proj_w), (norm_hbm, norm_gain), (mid_hbm, mid_gain),
        (gate_hbm, gate_w), (out_hbm, out_w),
    )
    loads = [pltpu.make_async_copy(*place, load_sem.at[n]) for n, place in enumerate(places)]
    for step in range(STEPS):
        rows = pl.ds(2 * step, 2)
        loads.append(
            pltpu.make_async_copy(pair_hbm.at[rows], pair.at[rows], load_sem.at[5 + step])
        )
    barrier = pltpu.get_barrier_semaphore()

    @pl.when(me != 0)
    def _():
        for offset in OFFSETS:
            pl.semaphore_signal(
                barrier, inc=1, device_id=(crop, towards(offset)), device_id_type=MESH
            )

    @pl.when(me == 0)
    def _():
        pl.semaphore_wait(barrier, len(OFFSETS))
        for offset in OFFSETS:
            pl.semaphore_signal(
                entered, inc=1, device_id=(crop, towards(offset)), device_id_type=MESH
            )

    for load in loads:
        load.start()

    members = [towards(offset) for offset in OFFSETS]

    def send_to(there, sem, source, target, cut=None):
        from_ref, to_ref = source.at[there], target.at[me]
        if cut is not None:
            from_ref, to_ref = from_ref.at[pl.ds(*cut)], to_ref.at[pl.ds(*cut)]
        pltpu.make_async_remote_copy(
            src_ref=from_ref,
            dst_ref=to_ref,
            send_sem=send_sem.at[sem],
            recv_sem=recv_sem.at[sem],
            device_id=(crop, there),
            device_id_type=MESH,
        ).start()

    def exchange(sem, source, target, cut=None):
        for there in members:
            send_to(there, sem, source, target, cut)

    def send_first(step):
        for part, *cut in PLAN[0].get(step, ()):
            for there in members:

                @pl.when(there != 0)
                def _():
                    send_to(there, part, send_proj.at[0, part], recv_proj.at[0, part], cut)

    def send_second(step):
        for part, *cut in PLAN[1].get(step, ()):
            exchange(4 + part, send_proj.at[1, part], recv_proj.at[1, part], cut)

    def all_of(sem, buffer):
        blocks = buffer.at[pl.ds(0, len(OFFSETS))]
        pltpu.make_async_copy(blocks, blocks, sem).wait()

    def column(row):
        return jnp.broadcast_to(row, (CHANS, CHANS)).T

    def pick(side):
        row = lax.broadcasted_iota(jnp.int32, (2 * CHANS, CHANS), 0)
        column_of = lax.broadcasted_iota(jnp.int32, (2 * CHANS, CHANS), 1)
        group, place = row // PART, lax.rem(row, PART)
        hit = (lax.rem(group, 2) == side) & (column_of == (group // 2) * PART + place)
        return jnp.where(hit, 0.5, 0.0).astype(BF16)

    for side in range(2):
        picks[side] = pick(side)

    def turn_projection(block):
        for kind in range(2):
            turned = jnp.zeros((2 * CHANS, CHANS), F32)
            for side in range(2):
                at = (2 * side + kind) * CHANS
                piece = proj_w[block, :, at : at + CHANS]
                turned = turned + contract(picks[side], piece, 1, 1)
            proj_t[block, kind] = turned.astype(BF16)

    def normalize(block, step, values):
        mean = jnp.mean(values, axis=0, keepdims=True)
        centered = values - mean
        var = jnp.mean(centered * centered, axis=0, keepdims=True)
        gain = gains[block]
        normed = centered * lax.rsqrt(var + 1e-05) * jnp.concatenate([gain, gain], axis=1)
        chan_normed[:, step * 256 : (step + 1) * 256] = normed.astype(BF16)

    def project(block, step):
        normed = chan_normed[:, step * 256 : (step + 1) * 256]
        for half in range(2):
            at = slice(half * CHANS, (half + 1) * CHANS)
            half_value = contract(proj_t[block, 0, at], normed, 1, 0)
            half_gate = contract(proj_t[block, 1, at], normed, 1, 0)
            sides = half_value * jnp.tanh(half_gate) + half_value
            rows = [
                sides[:, h * RES : (h + 1) * RES].reshape(GROUP // 2, 2, 2 * PART, RES)
                for h in range(2)
            ]
            both = jnp.concatenate(rows, axis=2).astype(BF16)
            owners = slice(half * GROUP // 2, (half + 1) * GROUP // 2)
            for part in range(2):
                send_proj[block, part, owners, step] = both[:, part]

    def keep_own(sent, received):
        received[me] = sent[me]

    def mix(block):
        over = 1 if block == 0 else 0
        size = 2 * PART * ROWS
        for part in range(2):
            all_of(recv_sem.at[4 * block + part], recv_proj.at[block, part])
            for origin in range(GROUP):
                wide_proj[part, origin * size : (origin + 1) * size, :] = (
                    recv_proj[block, part, origin].astype(F32).reshape(size, RES)
                )
            for pair_of in range(PART // 2):
                mixed = []
                for c in (2 * pair_of, 2 * pair_of + 1):
                    left = wide_proj[part, pl.ds(c, RES, stride=2 * PART), :].astype(BF16)
                    right = wide_proj[part, pl.ds(PART + c, RES, stride=2 * PART), :].astype(BF16)
                    mixed.append(contract(left, right, over, over).reshape(GROUP, ROWS, RES))
                send_mix[block, part, :, pair_of] = jnp.concatenate(mixed, axis=1).astype(BF16)
            exchange(4 * block + 2 + part, send_mix.at[block, part], recv_mix.at[block, part])
            keep_own(send_mix.at[block, part], recv_mix.at[block, part])

    def gather_mixed(block):
        size = OWN * ROWS
        total = jnp.zeros((ROWS, RES), F32)
        for part in range(2):
            all_of(recv_sem.at[4 * block + 2 + part], recv_mix.at[block, part])
            for origin in range(GROUP):
                values = recv_mix[block, part, origin].astype(F32).reshape(PART * ROWS, RES)
                at = origin * size + part * PART * ROWS
                wide_mix[at : at + PART * ROWS, :] = values
                total = total + jnp.sum(values.reshape(PART, ROWS, RES), axis=0)
        mean = total * (1.0 / CHANS)
        spread = jnp.zeros_like(mean)
        for origin in range(GROUP):
            values = wide_mix[origin * size : (origin + 1) * size, :].reshape(OWN, ROWS, RES) - mean
            spread = spread + jnp.sum(values * values, axis=0)
        stats[0] = mean
        stats[1] = lax.rsqrt(spread * (1.0 / CHANS) + 1e-05)

    def mid_row(block, i):
        values = wide_mix[pl.ds(i, CHANS, stride=ROWS), :]
        mean, scale = stats[0, i : i + 1, :], stats[1, i : i + 1, :]
        return ((values - mean) * scale * gains[2 + block]).astype(BF16)

    loads[1].wait()
    loads[0].wait()
    gains[0] = column(norm_gain[0:1, :])
    turn_projection(0)
    @pl.when(me != 0)
    def _():
        pl.semaphore_wait(barrier, len(OFFSETS) - 1)

    for first in range(0, STEPS, 2):
        steps = range(first, first + 2)
        for step in steps:
            loads[5 + step].wait()
            values = jnp.concatenate([pair[2 * step + h].astype(F32).T for h in range(2)], axis=1)
            chan_pair[:, step * 256 : (step + 1) * 256] = values
            normalize(0, step, values)
        for step in steps:
            project(0, step)
            send_first(step)

    @pl.when(me != 0)
    def _():
        pl.semaphore_wait(entered, 1)
        for part in range(2):
            send_to(0, part, send_proj.at[0, part], recv_proj.at[0, part])

    for part in range(2):
        keep_own(send_proj.at[0, part], recv_proj.at[0, part])

    for load in loads[2:5]:
        load.wait()
    gains[1] = column(norm_gain[1:2, :])
    gains[2] = column(mid_gain[0:1, :])
    gains[3] = column(mid_gain[1:2, :])
    turn_projection(1)
    gate_t[...] = (gate_w[0].astype(F32).T * 0.5).astype(BF16)
    out_t[...] = out_w[0].astype(F32).T.astype(BF16)
    for step in range(STEPS):
        at = slice(step * 256, (step + 1) * 256)
        chan_gate[:, at] = 0.5 * jnp.tanh(contract(gate_t[...], chan_normed[:, at], 1, 0)) + 0.5

    mix(0)
    gather_mixed(0)
    for first in range(0, STEPS, 2):
        steps = range(first, first + 2)
        for step in steps:
            at = slice(step * 256, (step + 1) * 256)
            mid = jnp.concatenate([mid_row(0, 2 * step), mid_row(0, 2 * step + 1)], axis=1)
            update = chan_gate[:, at] * contract(out_t[...], mid, 1, 0)
            values = (chan_pair[:, at] + update).astype(BF16).astype(F32)
            chan_pair[:, at] = values
            normalize(1, step, values)
        for step in steps:
            project(1, step)
            send_second(step)

    for part in range(2):
        keep_own(send_proj.at[1, part], recv_proj.at[1, part])
    half_gate_w = (gate_w[1].astype(F32) * 0.5).astype(BF16)
    for i in range(ROWS):
        at = slice(i * RES, (i + 1) * RES)
        row_gate[i] = 0.5 * jnp.tanh(contract(chan_normed[:, at], half_gate_w, 0, 0)) + 0.5
        row_pair[i] = chan_pair[:, at].T
    mix(1)
    gather_mixed(1)
    for i in range(ROWS):
        update = row_gate[i] * contract(mid_row(1, i), out_w[1], 0, 0)
        result[i] = (row_pair[i] + update).astype(BF16)

    for block in range(2):
        for part in range(2):
            all_of(send_sem.at[4 * block + part], send_proj.at[block, part])
            all_of(send_sem.at[4 * block + 2 + part], send_mix.at[block, part])


def per_device(pair_rep, proj_weight, gate_weight, out_weight, norm_gain, mid_gain):
    operands = (pair_rep, proj_weight, gate_weight, out_weight, norm_gain, mid_gain)
    operands = [pltpu.with_memory_space_constraint(value, pltpu.HBM) for value in operands]
    return pl.pallas_call(
        kernel,
        out_shape=jax.ShapeDtypeStruct((ROWS, RES, CHANS), BF16),
        in_specs=[pl.BlockSpec(memory_space=pltpu.HBM)] * 6,
        out_specs=pl.BlockSpec(memory_space=pltpu.VMEM),
        scratch_shapes=[
            pltpu.VMEM((ROWS, RES, CHANS), BF16),
            pltpu.VMEM((2, CHANS, 4 * CHANS), BF16),
            pltpu.VMEM((2, CHANS, CHANS), BF16),
            pltpu.VMEM((2, CHANS, CHANS), BF16),
            pltpu.VMEM((2, CHANS), F32),
            pltpu.VMEM((2, CHANS), F32),
            pltpu.SemaphoreType.DMA((5 + STEPS,)),
            pltpu.VMEM((2, 2 * CHANS, CHANS), BF16),
            pltpu.VMEM((2, 2, 2 * CHANS, CHANS), BF16),
            pltpu.VMEM((CHANS, CHANS), BF16),
            pltpu.VMEM((CHANS, CHANS), BF16),
            pltpu.VMEM((4, CHANS, CHANS), F32),
            pltpu.VMEM((CHANS, ROWS * RES), F32),
            pltpu.VMEM((CHANS, ROWS * RES), BF16),
            pltpu.VMEM((CHANS, ROWS * RES), F32),
            pltpu.VMEM((ROWS, RES, CHANS), F32),
            pltpu.VMEM((ROWS, RES, CHANS), F32),
            pltpu.VMEM((2, 2, GROUP, STEPS, 4 * PART, RES), BF16),
            pltpu.VMEM((2, 2, GROUP, STEPS, 4 * PART, RES), BF16),
            pltpu.VMEM((2, 2, GROUP, PART // 2, 2 * ROWS, RES), BF16),
            pltpu.VMEM((2, 2, GROUP, PART // 2, 2 * ROWS, RES), BF16),
            pltpu.VMEM((2, RES * 2 * PART, RES), F32),
            pltpu.VMEM((CHANS * ROWS, RES), F32),
            pltpu.VMEM((2, ROWS, RES), F32),
            pltpu.SemaphoreType.DMA((8,)),
            pltpu.SemaphoreType.DMA((8,)),
            pltpu.SemaphoreType.REGULAR,
        ],
        compiler_params=pltpu.CompilerParams(
            collective_id=0, has_side_effects=True, vmem_limit_bytes=32 * 1024 * 1024
        ),
        name="triangles",
    )(*operands)


def solution(mesh):
    return jax.shard_map(
        per_device,
        mesh=mesh,
        in_specs=(P(("dp", "dap"), None, None), P(), P(), P(), P(), P()),
        out_specs=P(("dp", "dap"), None, None),
        check_vma=False,
    )
```

```python
import jax
import jax.numpy as jnp
from jax import lax
from jax.experimental import pallas as pl
from jax.experimental.pallas import tpu as pltpu
from jax.sharding import PartitionSpec as P

MESH = pl.DeviceIdType.MESH
BF16 = jnp.bfloat16
F32 = jnp.float32
SIDE = 4
GROUP = SIDE * SIDE
RES = 128
CHANS = 128
ROWS = RES // GROUP
OWN = CHANS // GROUP
PART = OWN // 2
STEPS = ROWS // 2


def far_first(offset):
    return -sum(min(step, SIDE - step) for step in offset)


OFFSETS = sorted(
    [(dy, dx) for dy in range(SIDE) for dx in range(SIDE) if (dy, dx) != (0, 0)], key=far_first
)

PLAN = (
    {1: ((0, 0, 2),), 3: ((0, 2, 2), (1, 0, 4))},
    {1: ((0, 0, 2),), 3: ((0, 2, 2), (1, 0, 4))},
)


def contract(lhs, rhs, lhs_dim, rhs_dim):
    return lax.dot_general(
        lhs, rhs, (((lhs_dim,), (rhs_dim,)), ((), ())), preferred_element_type=F32
    )


def kernel(
    pair_hbm, proj_hbm, gate_hbm, out_hbm, norm_hbm, mid_hbm, result,
    pair, proj_w, gate_w, out_w, norm_gain, mid_gain, load_sem, picks, proj_t, gate_t, out_t, gains, chan_pair, chan_normed, chan_gate, row_gate, row_pair,
    send_proj, recv_proj, send_mix, recv_mix, wide_proj, wide_mix, stats, send_sem, recv_sem, entered,
):
    crop = lax.axis_index("dp")
    me = lax.axis_index("dap")
    y, x = me // SIDE, lax.rem(me, SIDE)

    def towards(offset):
        return lax.rem(y + offset[0], SIDE) * SIDE + lax.rem(x + offset[1], SIDE)

    places = (
        (proj_hbm, proj_w), (norm_hbm, norm_gain), (mid_hbm, mid_gain),
        (gate_hbm, gate_w), (out_hbm, out_w),
    )
    loads = [pltpu.make_async_copy(*place, load_sem.at[n]) for n, place in enumerate(places)]
    for step in range(STEPS):
        rows = pl.ds(2 * step, 2)
        loads.append(
            pltpu.make_async_copy(pair_hbm.at[rows], pair.at[rows], load_sem.at[5 + step])
        )
    barrier = pltpu.get_barrier_semaphore()

    @pl.when(me != 0)
    def _():
        for offset in OFFSETS:
            pl.semaphore_signal(
                barrier, inc=1, device_id=(crop, towards(offset)), device_id_type=MESH
            )

    @pl.when(me == 0)
    def _():
        pl.semaphore_wait(barrier, len(OFFSETS))
        for offset in OFFSETS:
            pl.semaphore_signal(
                entered, inc=1, device_id=(crop, towards(offset)), device_id_type=MESH
            )

    for load in loads:
        load.start()

    members = [towards(offset) for offset in OFFSETS]

    def send_to(there, sem, source, target, cut=None):
        from_ref, to_ref = source.at[there], target.at[me]
        if cut is not None:
            from_ref, to_ref = from_ref.at[pl.ds(*cut)], to_ref.at[pl.ds(*cut)]
        pltpu.make_async_remote_copy(
            src_ref=from_ref,
            dst_ref=to_ref,
            send_sem=send_sem.at[sem],
            recv_sem=recv_sem.at[sem],
            device_id=(crop, there),
            device_id_type=MESH,
        ).start()

    def exchange(sem, source, target, cut=None):
        for there in members:
            send_to(there, sem, source, target, cut)

    def send_first(step):
        for part, *cut in PLAN[0].get(step, ()):
            for there in members:

                @pl.when(there != 0)
                def _():
                    send_to(there, part, send_proj.at[0, part], recv_proj.at[0, part], cut)

    def send_second(step):
        for part, *cut in PLAN[1].get(step, ()):
            exchange(4 + part, send_proj.at[1, part], recv_proj.at[1, part], cut)

    def all_of(sem, buffer):
        blocks = buffer.at[pl.ds(0, len(OFFSETS))]
        pltpu.make_async_copy(blocks, blocks, sem).wait()

    def column(row):
        return jnp.broadcast_to(row, (CHANS, CHANS)).T

    def pick(side):
        row = lax.broadcasted_iota(jnp.int32, (2 * CHANS, CHANS), 0)
        column_of = lax.broadcasted_iota(jnp.int32, (2 * CHANS, CHANS), 1)
        group, place = row // PART, lax.rem(row, PART)
        hit = (lax.rem(group, 2) == side) & (column_of == (group // 2) * PART + place)
        return jnp.where(hit, 0.5, 0.0).astype(BF16)

    for side in range(2):
        picks[side] = pick(side)

    def turn_projection(block):
        for kind in range(2):
            turned = jnp.zeros((2 * CHANS, CHANS), F32)
            for side in range(2):
                at = (2 * side + kind) * CHANS
                piece = proj_w[block, :, at : at + CHANS]
                turned = turned + contract(picks[side], piece, 1, 1)
            proj_t[block, kind] = turned.astype(BF16)

    def normalize(block, step, values):
        mean = jnp.mean(values, axis=0, keepdims=True)
        centered = values - mean
        var = jnp.mean(centered * centered, axis=0, keepdims=True)
        gain = gains[block]
        normed = centered * lax.rsqrt(var + 1e-05) * jnp.concatenate([gain, gain], axis=1)
        chan_normed[:, step * 256 : (step + 1) * 256] = normed.astype(BF16)

    def project(block, step):
        normed = chan_normed[:, step * 256 : (step + 1) * 256]
        for half in range(2):
            at = slice(half * CHANS, (half + 1) * CHANS)
            half_value = contract(proj_t[block, 0, at], normed, 1, 0)
            half_gate = contract(proj_t[block, 1, at], normed, 1, 0)
            sides = half_value * jnp.tanh(half_gate) + half_value
            rows = [
                sides[:, h * RES : (h + 1) * RES].reshape(GROUP // 2, 2, 2 * PART, RES)
                for h in range(2)
            ]
            both = jnp.concatenate(rows, axis=2).astype(BF16)
            owners = slice(half * GROUP // 2, (half + 1) * GROUP // 2)
            for part in range(2):
                send_proj[block, part, owners, step] = both[:, part]

    def keep_own(sent, received):
        received[me] = sent[me]

    def mix(block):
        over = 1 if block == 0 else 0
        size = 2 * PART * ROWS
        for part in range(2):
            all_of(recv_sem.at[4 * block + part], recv_proj.at[block, part])
            for origin in range(GROUP):
                wide_proj[part, origin * size : (origin + 1) * size, :] = (
                    recv_proj[block, part, origin].astype(F32).reshape(size, RES)
                )
            for pair_of in range(PART // 2):
                mixed = []
                for c in (2 * pair_of, 2 * pair_of + 1):
                    left = wide_proj[part, pl.ds(c, RES, stride=2 * PART), :].astype(BF16)
                    right = wide_proj[part, pl.ds(PART + c, RES, stride=2 * PART), :].astype(BF16)
                    mixed.append(contract(left, right, over, over).reshape(GROUP, ROWS, RES))
                send_mix[block, part, :, pair_of] = jnp.concatenate(mixed, axis=1).astype(BF16)
            exchange(4 * block + 2 + part, send_mix.at[block, part], recv_mix.at[block, part])
            keep_own(send_mix.at[block, part], recv_mix.at[block, part])

    def gather_mixed(block):
        size = OWN * ROWS
        total = jnp.zeros((ROWS, RES), F32)
        for part in range(2):
            all_of(recv_sem.at[4 * block + 2 + part], recv_mix.at[block, part])
            for origin in range(GROUP):
                values = recv_mix[block, part, origin].astype(F32).reshape(PART * ROWS, RES)
                at = origin * size + part * PART * ROWS
                wide_mix[at : at + PART * ROWS, :] = values
                total = total + jnp.sum(values.reshape(PART, ROWS, RES), axis=0)
        mean = total * (1.0 / CHANS)
        spread = jnp.zeros_like(mean)
        for origin in range(GROUP):
            values = wide_mix[origin * size : (origin + 1) * size, :].reshape(OWN, ROWS, RES) - mean
            spread = spread + jnp.sum(values * values, axis=0)
        stats[0] = mean
        stats[1] = lax.rsqrt(spread * (1.0 / CHANS) + 1e-05)

    def mid_row(block, i):
        values = wide_mix[pl.ds(i, CHANS, stride=ROWS), :]
        mean, scale = stats[0, i : i + 1, :], stats[1, i : i + 1, :]
        return ((values - mean) * scale * gains[2 + block]).astype(BF16)

    loads[1].wait()
    loads[0].wait()
    gains[0] = column(norm_gain[0:1, :])
    turn_projection(0)
    @pl.when(me != 0)
    def _():
        pl.semaphore_wait(barrier, len(OFFSETS) - 1)

    for first in range(0, STEPS, 2):
        steps = range(first, first + 2)
        for step in steps:
            loads[5 + step].wait()
            values = jnp.concatenate([pair[2 * step + h].astype(F32).T for h in range(2)], axis=1)
            chan_pair[:, step * 256 : (step + 1) * 256] = values
            normalize(0, step, values)
        for step in steps:
            project(0, step)
            send_first(step)

    @pl.when(me != 0)
    def _():
        pl.semaphore_wait(entered, 1)
        for part in range(2):
            send_to(0, part, send_proj.at[0, part], recv_proj.at[0, part])

    for part in range(2):
        keep_own(send_proj.at[0, part], recv_proj.at[0, part])

    for load in loads[2:5]:
        load.wait()
    gains[1] = column(norm_gain[1:2, :])
    gains[2] = column(mid_gain[0:1, :])
    gains[3] = column(mid_gain[1:2, :])
    turn_projection(1)
    gate_t[...] = (gate_w[0].astype(F32).T * 0.5).astype(BF16)
    out_t[...] = out_w[0].astype(F32).T.astype(BF16)
    for step in range(STEPS):
        at = slice(step * 256, (step + 1) * 256)
        chan_gate[:, at] = 0.5 * jnp.tanh(contract(gate_t[...], chan_normed[:, at], 1, 0)) + 0.5

    mix(0)
    gather_mixed(0)
    for first in range(0, STEPS, 2):
        steps = range(first, first + 2)
        for step in steps:
            at = slice(step * 256, (step + 1) * 256)
            mid = jnp.concatenate([mid_row(0, 2 * step), mid_row(0, 2 * step + 1)], axis=1)
            update = chan_gate[:, at] * contract(out_t[...], mid, 1, 0)
            values = (chan_pair[:, at] + update).astype(BF16).astype(F32)
            chan_pair[:, at] = values
            normalize(1, step, values)
        for step in steps:
            project(1, step)
            send_second(step)

    for part in range(2):
        keep_own(send_proj.at[1, part], recv_proj.at[1, part])
    half_gate_w = (gate_w[1].astype(F32) * 0.5).astype(BF16)
    for i in range(ROWS):
        at = slice(i * RES, (i + 1) * RES)
        row_gate[i] = 0.5 * jnp.tanh(contract(chan_normed[:, at], half_gate_w, 0, 0)) + 0.5
        row_pair[i] = chan_pair[:, at].T
    mix(1)
    gather_mixed(1)
    for i in range(ROWS):
        update = row_gate[i] * contract(mid_row(1, i), out_w[1], 0, 0)
        result[i] = (row_pair[i] + update).astype(BF16)

    for block in range(2):
        for part in range(2):
            all_of(send_sem.at[4 * block + part], send_proj.at[block, part])
            all_of(send_sem.at[4 * block + 2 + part], send_mix.at[block, part])


def per_device(pair_rep, proj_weight, gate_weight, out_weight, norm_gain, mid_gain):
    operands = (pair_rep, proj_weight, gate_weight, out_weight, norm_gain, mid_gain)
    operands = [pltpu.with_memory_space_constraint(value, pltpu.HBM) for value in operands]
    return pl.pallas_call(
        kernel,
        out_shape=jax.ShapeDtypeStruct((ROWS, RES, CHANS), BF16),
        in_specs=[pl.BlockSpec(memory_space=pltpu.HBM)] * 6,
        out_specs=pl.BlockSpec(memory_space=pltpu.VMEM),
        scratch_shapes=[
            pltpu.VMEM((ROWS, RES, CHANS), BF16),
            pltpu.VMEM((2, CHANS, 4 * CHANS), BF16),
            pltpu.VMEM((2, CHANS, CHANS), BF16),
            pltpu.VMEM((2, CHANS, CHANS), BF16),
            pltpu.VMEM((2, CHANS), F32),
            pltpu.VMEM((2, CHANS), F32),
            pltpu.SemaphoreType.DMA((5 + STEPS,)),
            pltpu.VMEM((2, 2 * CHANS, CHANS), BF16),
            pltpu.VMEM((2, 2, 2 * CHANS, CHANS), BF16),
            pltpu.VMEM((CHANS, CHANS), BF16),
            pltpu.VMEM((CHANS, CHANS), BF16),
            pltpu.VMEM((4, CHANS, CHANS), F32),
            pltpu.VMEM((CHANS, ROWS * RES), F32),
            pltpu.VMEM((CHANS, ROWS * RES), BF16),
            pltpu.VMEM((CHANS, ROWS * RES), F32),
            pltpu.VMEM((ROWS, RES, CHANS), F32),
            pltpu.VMEM((ROWS, RES, CHANS), F32),
            pltpu.VMEM((2, 2, GROUP, STEPS, 4 * PART, RES), BF16),
            pltpu.VMEM((2, 2, GROUP, STEPS, 4 * PART, RES), BF16),
            pltpu.VMEM((2, 2, GROUP, PART // 2, 2 * ROWS, RES), BF16),
            pltpu.VMEM((2, 2, GROUP, PART // 2, 2 * ROWS, RES), BF16),
            pltpu.VMEM((2, RES * 2 * PART, RES), F32),
            pltpu.VMEM((CHANS * ROWS, RES), F32),
            pltpu.VMEM((2, ROWS, RES), F32),
            pltpu.SemaphoreType.DMA((8,)),
            pltpu.SemaphoreType.DMA((8,)),
            pltpu.SemaphoreType.REGULAR,
        ],
        compiler_params=pltpu.CompilerParams(
            collective_id=0, has_side_effects=True, vmem_limit_bytes=32 * 1024 * 1024
        ),
        name="triangles",
    )(*operands)


def solution(mesh):
    return jax.shard_map(
        per_device,
        mesh=mesh,
        in_specs=(P(("dp", "dap"), None, None), P(), P(), P(), P(), P()),
        out_specs=P(("dp", "dap"), None, None),
        check_vma=False,
    )
```

```python
import jax
import jax.numpy as jnp
from jax import lax
from jax.experimental import pallas as pl
from jax.experimental.pallas import tpu as pltpu
from jax.sharding import PartitionSpec as P

MESH = pl.DeviceIdType.MESH
BF16 = jnp.bfloat16
F32 = jnp.float32
SIDE = 4
GROUP = SIDE * SIDE
RES = 128
CHANS = 128
ROWS = RES // GROUP
OWN = CHANS // GROUP
PART = OWN // 2
STEPS = ROWS // 2


def far_first(offset):
    return -sum(min(step, SIDE - step) for step in offset)


OFFSETS = sorted(
    [(dy, dx) for dy in range(SIDE) for dx in range(SIDE) if (dy, dx) != (0, 0)], key=far_first
)

PLAN = (
    {1: ((0, 0, 2),), 3: ((0, 2, 2), (1, 0, 4))},
    {1: ((0, 0, 2),), 3: ((0, 2, 2), (1, 0, 4))},
)


def contract(lhs, rhs, lhs_dim, rhs_dim):
    return lax.dot_general(
        lhs, rhs, (((lhs_dim,), (rhs_dim,)), ((), ())), preferred_element_type=F32
    )


def kernel(
    pair_hbm, proj_hbm, gate_hbm, out_hbm, norm_hbm, mid_hbm, result,
    pair, proj_w, gate_w, out_w, norm_gain, mid_gain, load_sem, picks, proj_t, gate_t, out_t, gains, chan_pair, chan_normed, chan_gate, row_gate, row_pair,
    send_proj, recv_proj, send_mix, recv_mix, wide_proj, wide_mix, stats, send_sem, recv_sem, entered,
):
    crop = lax.axis_index("dp")
    me = lax.axis_index("dap")
    y, x = me // SIDE, lax.rem(me, SIDE)

    def towards(offset):
        return lax.rem(y + offset[0], SIDE) * SIDE + lax.rem(x + offset[1], SIDE)

    places = (
        (proj_hbm, proj_w), (norm_hbm, norm_gain), (mid_hbm, mid_gain),
        (gate_hbm, gate_w), (out_hbm, out_w),
    )
    loads = [pltpu.make_async_copy(*place, load_sem.at[n]) for n, place in enumerate(places)]
    for step in range(STEPS):
        rows = pl.ds(2 * step, 2)
        loads.append(
            pltpu.make_async_copy(pair_hbm.at[rows], pair.at[rows], load_sem.at[5 + step])
        )
    for load in loads[:2] + loads[5:]:
        load.start()

    barrier = pltpu.get_barrier_semaphore()

    @pl.when(me != 0)
    def _():
        for offset in OFFSETS:
            pl.semaphore_signal(
                barrier, inc=1, device_id=(crop, towards(offset)), device_id_type=MESH
            )

    @pl.when(me == 0)
    def _():
        pl.semaphore_wait(barrier, len(OFFSETS))
        for offset in OFFSETS:
            pl.semaphore_signal(
                entered, inc=1, device_id=(crop, towards(offset)), device_id_type=MESH
            )

    for load in loads[2:5]:
        load.start()

    members = [towards(offset) for offset in OFFSETS]

    def send_to(there, sem, source, target, cut=None):
        from_ref, to_ref = source.at[there], target.at[me]
        if cut is not None:
            from_ref, to_ref = from_ref.at[pl.ds(*cut)], to_ref.at[pl.ds(*cut)]
        pltpu.make_async_remote_copy(
            src_ref=from_ref,
            dst_ref=to_ref,
            send_sem=send_sem.at[sem],
            recv_sem=recv_sem.at[sem],
            device_id=(crop, there),
            device_id_type=MESH,
        ).start()

    def exchange(sem, source, target, cut=None):
        for there in members:
            send_to(there, sem, source, target, cut)

    def send_first(step):
        for part, *cut in PLAN[0].get(step, ()):
            for there in members:

                @pl.when(there != 0)
                def _():
                    send_to(there, part, send_proj.at[0, part], recv_proj.at[0, part], cut)

    def send_second(step):
        for part, *cut in PLAN[1].get(step, ()):
            exchange(4 + part, send_proj.at[1, part], recv_proj.at[1, part], cut)

    def all_of(sem, buffer):
        blocks = buffer.at[pl.ds(0, len(OFFSETS))]
        pltpu.make_async_copy(blocks, blocks, sem).wait()

    def column(row):
        return jnp.broadcast_to(row, (CHANS, CHANS)).T

    def pick(side):
        row = lax.broadcasted_iota(jnp.int32, (2 * CHANS, CHANS), 0)
        column_of = lax.broadcasted_iota(jnp.int32, (2 * CHANS, CHANS), 1)
        group, place = row // PART, lax.rem(row, PART)
        hit = (lax.rem(group, 2) == side) & (column_of == (group // 2) * PART + place)
        return jnp.where(hit, 0.5, 0.0).astype(BF16)

    for side in range(2):
        picks[side] = pick(side)

    def turn_projection(block):
        for kind in range(2):
            turned = jnp.zeros((2 * CHANS, CHANS), F32)
            for side in range(2):
                at = (2 * side + kind) * CHANS
                piece = proj_w[block, :, at : at + CHANS]
                turned = turned + contract(picks[side], piece, 1, 1)
            proj_t[block, kind] = turned.astype(BF16)

    def normalize(block, step, values):
        mean = jnp.mean(values, axis=0, keepdims=True)
        centered = values - mean
        var = jnp.mean(centered * centered, axis=0, keepdims=True)
        gain = gains[block]
        normed = centered * lax.rsqrt(var + 1e-05) * jnp.concatenate([gain, gain], axis=1)
        chan_normed[:, step * 256 : (step + 1) * 256] = normed.astype(BF16)

    def project(block, step):
        normed = chan_normed[:, step * 256 : (step + 1) * 256]
        for half in range(2):
            at = slice(half * CHANS, (half + 1) * CHANS)
            half_value = contract(proj_t[block, 0, at], normed, 1, 0)
            half_gate = contract(proj_t[block, 1, at], normed, 1, 0)
            sides = half_value * jnp.tanh(half_gate) + half_value
            rows = [
                sides[:, h * RES : (h + 1) * RES].reshape(GROUP // 2, 2, 2 * PART, RES)
                for h in range(2)
            ]
            both = jnp.concatenate(rows, axis=2).astype(BF16)
            owners = slice(half * GROUP // 2, (half + 1) * GROUP // 2)
            for part in range(2):
                send_proj[block, part, owners, step] = both[:, part]

    def keep_own(sent, received):
        received[me] = sent[me]

    def mix(block):
        over = 1 if block == 0 else 0
        size = 2 * PART * ROWS
        for part in range(2):
            all_of(recv_sem.at[4 * block + part], recv_proj.at[block, part])
            for origin in range(GROUP):
                wide_proj[part, origin * size : (origin + 1) * size, :] = (
                    recv_proj[block, part, origin].astype(F32).reshape(size, RES)
                )
            for pair_of in range(PART // 2):
                mixed = []
                for c in (2 * pair_of, 2 * pair_of + 1):
                    left = wide_proj[part, pl.ds(c, RES, stride=2 * PART), :].astype(BF16)
                    right = wide_proj[part, pl.ds(PART + c, RES, stride=2 * PART), :].astype(BF16)
                    mixed.append(contract(left, right, over, over).reshape(GROUP, ROWS, RES))
                send_mix[block, part, :, pair_of] = jnp.concatenate(mixed, axis=1).astype(BF16)
            exchange(4 * block + 2 + part, send_mix.at[block, part], recv_mix.at[block, part])
            keep_own(send_mix.at[block, part], recv_mix.at[block, part])

    def gather_mixed(block):
        size = OWN * ROWS
        total = jnp.zeros((ROWS, RES), F32)
        for part in range(2):
            all_of(recv_sem.at[4 * block + 2 + part], recv_mix.at[block, part])
            for origin in range(GROUP):
                values = recv_mix[block, part, origin].astype(F32).reshape(PART * ROWS, RES)
                at = origin * size + part * PART * ROWS
                wide_mix[at : at + PART * ROWS, :] = values
                total = total + jnp.sum(values.reshape(PART, ROWS, RES), axis=0)
        mean = total * (1.0 / CHANS)
        spread = jnp.zeros_like(mean)
        for origin in range(GROUP):
            values = wide_mix[origin * size : (origin + 1) * size, :].reshape(OWN, ROWS, RES) - mean
            spread = spread + jnp.sum(values * values, axis=0)
        stats[0] = mean
        stats[1] = lax.rsqrt(spread * (1.0 / CHANS) + 1e-05)

    def mid_row(block, i):
        values = wide_mix[pl.ds(i, CHANS, stride=ROWS), :]
        mean, scale = stats[0, i : i + 1, :], stats[1, i : i + 1, :]
        return ((values - mean) * scale * gains[2 + block]).astype(BF16)

    loads[1].wait()
    loads[0].wait()
    gains[0] = column(norm_gain[0:1, :])
    turn_projection(0)
    @pl.when(me != 0)
    def _():
        pl.semaphore_wait(barrier, len(OFFSETS) - 1)

    for first in range(0, STEPS, 2):
        steps = range(first, first + 2)
        for step in steps:
            loads[5 + step].wait()
            values = jnp.concatenate([pair[2 * step + h].astype(F32).T for h in range(2)], axis=1)
            chan_pair[:, step * 256 : (step + 1) * 256] = values
            normalize(0, step, values)
        for step in steps:
            project(0, step)
            send_first(step)

    @pl.when(me != 0)
    def _():
        pl.semaphore_wait(entered, 1)
        for part in range(2):
            send_to(0, part, send_proj.at[0, part], recv_proj.at[0, part])

    for part in range(2):
        keep_own(send_proj.at[0, part], recv_proj.at[0, part])

    for load in loads[2:5]:
        load.wait()
    gains[1] = column(norm_gain[1:2, :])
    gains[2] = column(mid_gain[0:1, :])
    gains[3] = column(mid_gain[1:2, :])
    turn_projection(1)
    gate_t[...] = (gate_w[0].astype(F32).T * 0.5).astype(BF16)
    out_t[...] = out_w[0].astype(F32).T.astype(BF16)
    for step in range(STEPS):
        at = slice(step * 256, (step + 1) * 256)
        chan_gate[:, at] = 0.5 * jnp.tanh(contract(gate_t[...], chan_normed[:, at], 1, 0)) + 0.5

    mix(0)
    gather_mixed(0)
    for first in range(0, STEPS, 2):
        steps = range(first, first + 2)
        for step in steps:
            at = slice(step * 256, (step + 1) * 256)
            mid = jnp.concatenate([mid_row(0, 2 * step), mid_row(0, 2 * step + 1)], axis=1)
            update = chan_gate[:, at] * contract(out_t[...], mid, 1, 0)
            values = (chan_pair[:, at] + update).astype(BF16).astype(F32)
            chan_pair[:, at] = values
            normalize(1, step, values)
        for step in steps:
            project(1, step)
            send_second(step)

    for part in range(2):
        keep_own(send_proj.at[1, part], recv_proj.at[1, part])
    half_gate_w = (gate_w[1].astype(F32) * 0.5).astype(BF16)
    for i in range(ROWS):
        at = slice(i * RES, (i + 1) * RES)
        row_gate[i] = 0.5 * jnp.tanh(contract(chan_normed[:, at], half_gate_w, 0, 0)) + 0.5
        row_pair[i] = chan_pair[:, at].T
    mix(1)
    gather_mixed(1)
    for i in range(ROWS):
        update = row_gate[i] * contract(mid_row(1, i), out_w[1], 0, 0)
        result[i] = (row_pair[i] + update).astype(BF16)

    for block in range(2):
        for part in range(2):
            all_of(send_sem.at[4 * block + part], send_proj.at[block, part])
            all_of(send_sem.at[4 * block + 2 + part], send_mix.at[block, part])


def per_device(pair_rep, proj_weight, gate_weight, out_weight, norm_gain, mid_gain):
    operands = (pair_rep, proj_weight, gate_weight, out_weight, norm_gain, mid_gain)
    operands = [pltpu.with_memory_space_constraint(value, pltpu.HBM) for value in operands]
    return pl.pallas_call(
        kernel,
        out_shape=jax.ShapeDtypeStruct((ROWS, RES, CHANS), BF16),
        in_specs=[pl.BlockSpec(memory_space=pltpu.HBM)] * 6,
        out_specs=pl.BlockSpec(memory_space=pltpu.VMEM),
        scratch_shapes=[
            pltpu.VMEM((ROWS, RES, CHANS), BF16),
            pltpu.VMEM((2, CHANS, 4 * CHANS), BF16),
            pltpu.VMEM((2, CHANS, CHANS), BF16),
            pltpu.VMEM((2, CHANS, CHANS), BF16),
            pltpu.VMEM((2, CHANS), F32),
            pltpu.VMEM((2, CHANS), F32),
            pltpu.SemaphoreType.DMA((5 + STEPS,)),
            pltpu.VMEM((2, 2 * CHANS, CHANS), BF16),
            pltpu.VMEM((2, 2, 2 * CHANS, CHANS), BF16),
            pltpu.VMEM((CHANS, CHANS), BF16),
            pltpu.VMEM((CHANS, CHANS), BF16),
            pltpu.VMEM((4, CHANS, CHANS), F32),
            pltpu.VMEM((CHANS, ROWS * RES), F32),
            pltpu.VMEM((CHANS, ROWS * RES), BF16),
            pltpu.VMEM((CHANS, ROWS * RES), F32),
            pltpu.VMEM((ROWS, RES, CHANS), F32),
            pltpu.VMEM((ROWS, RES, CHANS), F32),
            pltpu.VMEM((2, 2, GROUP, STEPS, 4 * PART, RES), BF16),
            pltpu.VMEM((2, 2, GROUP, STEPS, 4 * PART, RES), BF16),
            pltpu.VMEM((2, 2, GROUP, PART // 2, 2 * ROWS, RES), BF16),
            pltpu.VMEM((2, 2, GROUP, PART // 2, 2 * ROWS, RES), BF16),
            pltpu.VMEM((2, RES * 2 * PART, RES), F32),
            pltpu.VMEM((CHANS * ROWS, RES), F32),
            pltpu.VMEM((2, ROWS, RES), F32),
            pltpu.SemaphoreType.DMA((8,)),
            pltpu.SemaphoreType.DMA((8,)),
            pltpu.SemaphoreType.REGULAR,
        ],
        compiler_params=pltpu.CompilerParams(
            collective_id=0, has_side_effects=True, vmem_limit_bytes=32 * 1024 * 1024
        ),
        name="triangles",
    )(*operands)


def solution(mesh):
    return jax.shard_map(
        per_device,
        mesh=mesh,
        in_specs=(P(("dp", "dap"), None, None), P(), P(), P(), P(), P()),
        out_specs=P(("dp", "dap"), None, None),
        check_vma=False,
    )
```
